256 devices in a mesh: seq: 32 (over x, z), tp: 8 (over y, core).
Axes of the slice: x: 4, y: 4, z: 8, core: 2. Of those that a mesh axis runs over, the one named last changes fastest.
Arguments:
- mixer_input: bfloat16 [8192, 16384], P('seq', 'tp'), may hold values from -512 to 512
- mixer_gate: bfloat16 [8192, 16384], P('seq', 'tp'), may hold values from -5 to 5
- state_write: bfloat16 [8192, 128], P('seq'), may hold values from -6 to 6
- state_read: bfloat16 [8192, 128], P('seq'), may hold values from -0.5 to 0.5
- log_decay: float32 [128, 8192], P('tp', 'seq'), may hold values from -1 to 0
- norm_gain: float32 [16384], P('tp'), may hold values from 0.1 to 1.9
- queries: bfloat16 [8192, 8192], P('seq', 'tp'), may hold values from -25 to 25
- key_matrix_rows: bfloat16 [8192, 1024], P('seq', 'tp'), may hold values from -25 to 25
- value_matrix_rows: bfloat16 [8192, 1024], P('seq', 'tp'), may hold values from -6 to 6
- request_blocks: int32 [4], replicated, may hold values from 1 to 32, as said below
Outputs:
- mixer_out: bfloat16 [8192, 16384], P('seq', 'tp')
- attention_out: bfloat16 [8192, 8192], P('seq', 'tp')
The draws below stay inside these ranges and needn't reach their ends.
Inputs may be any that keep to these rules, and one draw needn't show every extreme that they name: `request_blocks`: requests are packed in order and fill the sequence; the second request holds exactly 32 blocks.
All inputs are finite; a program needn't handle non-finite values.
Results may differ from the reference program's by a relative error of at most 0.011.
Values may be sent and summed in bfloat16 or wider, within the bound.
No kernel may reach another device: no remote copies, remote signals or barrier semaphores. Data moves between devices by JAX's collectives and lax.ppermute only.
A program may use at most 128 MiB of HBM per device.

```python
import math
import jax
import jax.numpy as jnp
from jax import lax

HEADS = 128
P_SIZE = 128
N = 128
QUERY_HEAD_COUNT = 64
KEY_VALUE_HEADS = 8
HEAD_WIDTH = 128
SEGMENT_SIZE = 256
CYCLE = 4
MOST_SLABS = 16
JOINED_SIZE = 8192
BLOCKS = 64
MOST_BLOCKS = 32
N_SEQ = 32


def attention_pair(key):
    random_query_draw = jnp.clip(jax.random.normal(jax.random.fold_in(key, 101), (JOINED_SIZE, QUERY_HEAD_COUNT * HEAD_WIDTH), jnp.float32), -5.0, 5.0)
    random_key_draw = jnp.clip(jax.random.normal(jax.random.fold_in(key, 102), (JOINED_SIZE, KEY_VALUE_HEADS * HEAD_WIDTH), jnp.float32), -5.0, 5.0)
    return (random_query_draw, random_key_draw)


def draw_queries(key, part):
    return attention_pair(key)[0].astype(jnp.bfloat16)


def draw_key_matrix_rows(key, part):
    return attention_pair(key)[1].astype(jnp.bfloat16)


def draw_request_blocks(key, part):
    remaining = BLOCKS - MOST_BLOCKS
    first_len = jax.random.randint(jax.random.fold_in(key, 401), (), 1, remaining - 1)
    third_len = jax.random.randint(jax.random.fold_in(key, 402), (), 1, remaining - first_len)
    fourth_len = remaining - first_len - third_len
    return jnp.stack([first_len, jnp.asarray(MOST_BLOCKS, jnp.int32), third_len, fourth_len]).astype(jnp.int32)


def draw_mixer_input(key, part):
    noise = jnp.clip(jax.random.normal(jax.random.fold_in(key, 201), (JOINED_SIZE, HEADS, P_SIZE), jnp.float32), -4.0, 4.0)
    ramp_top = 4.0
    head_scale = ramp_top ** (jnp.arange(HEADS, dtype=jnp.float32) / (HEADS - 1))
    channel_scale = jnp.exp(jax.random.uniform(jax.random.fold_in(key, 202), (HEADS, P_SIZE), jnp.float32, 0.0, math.log(2.5)))
    row_scale = jnp.exp(jax.random.uniform(jax.random.fold_in(key, 203), (JOINED_SIZE,), jnp.float32, math.log(1.0 / 3.0), math.log(10.0 / 3.0)))
    payload_array = noise * head_scale[None, :, None] * channel_scale[None] * row_scale[:, None, None]
    return payload_array.reshape(JOINED_SIZE, HEADS * P_SIZE).astype(jnp.bfloat16)


def draw_log_decay(key, part):
    chain_tokens = MOST_SLABS * SEGMENT_SIZE
    fast_cut = 4
    is_fast = jax.random.randint(jax.random.fold_in(key, 301), (HEADS,), 0, 8) < fast_cut
    fast_rate = 1.0 / jax.random.uniform(jax.random.fold_in(key, 302), (HEADS,), jnp.float32, 30.0, 50.0)
    slow_rate = jnp.exp(jax.random.uniform(jax.random.fold_in(key, 303), (HEADS,), jnp.float32, math.log(0.02), math.log(0.2))) / chain_tokens
    fading_speed = jnp.where(is_fast, fast_rate, slow_rate)
    slab_factor = jnp.exp(jax.random.uniform(jax.random.fold_in(key, 304), (HEADS, N_SEQ), jnp.float32, math.log(0.5), math.log(2.0)))
    slice_lines = jnp.repeat(slab_factor, SEGMENT_SIZE, axis=1)
    approximate_guess = jax.random.uniform(jax.random.fold_in(key, 305), (HEADS, JOINED_SIZE), jnp.float32, 0.5, 1.5)
    run_extent = jax.random.randint(jax.random.fold_in(key, 306), (JOINED_SIZE,), 0, 4 * SEGMENT_SIZE) == 0
    stack_level = jax.random.uniform(jax.random.fold_in(key, 307), (JOINED_SIZE,), jnp.float32, 0.5, 0.8)
    payload_array = -fading_speed[:, None] * slice_lines * approximate_guess + jnp.where(run_extent, jnp.log(stack_level), 0.0)[None, :]
    return payload_array.astype(jnp.float32)


def block_scale(stream_key, shape, cuts, least, high):
    def one(position, blocks):
        heights = jax.random.uniform(jax.random.fold_in(jax.random.fold_in(stream_key, 6), position), (blocks,), jnp.float32, least / len(cuts), high / len(cuts))
        return jnp.repeat(jnp.exp(heights), shape[position] // blocks).reshape((-1,) + (1,) * (len(shape) - position - 1))

    gain = one(*cuts[0])
    for cut in cuts[1:]:
        gain = gain * one(*cut)
    return gain


def centred(stream_key, extent, deviation, limit, shards=(), held_as=jnp.bfloat16):
    factor_of = block_scale(stream_key, extent, shards, -0.22, 0.18) if shards else 1.0
    array = jax.random.normal(stream_key, extent, jnp.float32) * deviation * factor_of
    return jnp.minimum(jnp.maximum(array, -limit), limit).astype(held_as)


def setup_inputs(seed: int = 0) -> dict:
    splits = jax.random.split(jax.random.key(seed), 11)
    return {
        "mixer_input": draw_mixer_input(jax.random.fold_in(splits[10], 71), 0),
        "mixer_gate": centred(splits[1], (JOINED_SIZE, HEADS * P_SIZE), 1.0, 5.0, ((0, 32), (1, 8))),
        "state_write": centred(splits[2], (JOINED_SIZE, N), 1.0, 6.0, ((0, 32),)),
        "state_read": centred(splits[3], (JOINED_SIZE, N), 0.09, 0.5, ((0, 32),)),
        "log_decay": draw_log_decay(jax.random.fold_in(splits[10], 71), 0),
        "norm_gain": jnp.clip(1.0 + 0.18 * jax.random.normal(splits[5], (HEADS * P_SIZE,), jnp.float32), 0.1, 1.9),
        "queries": draw_queries(jax.random.fold_in(splits[10], 71), 0),
        "key_matrix_rows": draw_key_matrix_rows(jax.random.fold_in(splits[10], 71), 0),
        "value_matrix_rows": centred(splits[8], (JOINED_SIZE, KEY_VALUE_HEADS * HEAD_WIDTH), 1.0, 6.0, ((0, 32), (1, 8))),
        "request_blocks": draw_request_blocks(jax.random.fold_in(splits[10], 71), 0),
    }


def segment_ids(request_blocks, positions):
    request_ends = jnp.cumsum(request_blocks).astype(jnp.int32) * 128
    counted = lax.optimization_barrier(jnp.sum((positions[:, None] >= request_ends[None, :]).astype(jnp.int32), axis=1))
    return jnp.where(positions < 0, -1, counted).astype(jnp.int32)

def mixer_part(mixer_input, mixer_gate, state_write, state_read, log_decay, norm_gain, segment):
    block_count = JOINED_SIZE // 128
    inputs = mixer_input.reshape(block_count, 128, HEADS, P_SIZE)
    gates = mixer_gate.reshape(block_count, 128, HEADS, P_SIZE)
    writes = state_write.reshape(block_count, 128, N)
    read_rows = state_read.reshape(block_count, 128, N)
    decays = log_decay.reshape(HEADS, block_count, 128).transpose(1, 0, 2)
    labels = segment.reshape(block_count, 128)
    before = jnp.concatenate([jnp.full((1,), -1, jnp.int32), labels[:-1, -1]]).astype(jnp.int32)
    causal = jnp.tril(jnp.ones((128, 128), dtype=bool))

    def advance(running_state, item):
        block_inputs, block_gates, block_writes, block_reads, block_decays, block_labels, label_before = item
        running = jnp.cumsum(block_decays, axis=1)
        shared = ((block_labels[:, None] == block_labels[None, :]) & causal)[None]
        spread = jnp.where(shared, running[:, :, None] - running[:, None, :], 0.0)
        weight = jnp.where(shared, jnp.exp(spread), 0.0)
        affinity = jnp.dot(block_reads, block_writes.T, preferred_element_type=jnp.float32)
        mixing = lax.optimization_barrier((weight * affinity[None]).astype(jnp.bfloat16))
        within = jnp.einsum('hij,jhp->ihp', mixing.astype(jnp.float32), block_inputs.astype(jnp.float32))
        opened = block_labels == label_before
        entry_decay = jnp.where(opened[None, :], jnp.exp(running), 0.0)
        from_state = jnp.einsum('in,hnp->ihp', block_reads.astype(jnp.float32), running_state, precision=lax.Precision.HIGHEST)
        mixed = within + from_state * entry_decay.T[:, :, None]
        gated = mixed * jax.nn.silu(block_gates.astype(jnp.float32))
        mean_square = lax.optimization_barrier(jnp.mean(gated * gated, axis=(1, 2)))
        scaling = lax.rsqrt(mean_square + 1e-05)
        block_out = ((gated * scaling[:, None, None]).reshape(128, HEADS * P_SIZE) * norm_gain[None, :]).astype(jnp.bfloat16)
        reaching = jnp.where((block_labels == block_labels[-1])[None, :], jnp.exp(running[:, -1:] - running), 0.0)
        carried = lax.optimization_barrier((block_inputs.astype(jnp.float32) * reaching.T[:, :, None]).astype(jnp.bfloat16))
        block_state = jnp.einsum('jn,jhp->hnp', block_writes.astype(jnp.float32), carried.astype(jnp.float32))
        block_decay = jnp.where(opened[-1], jnp.exp(running[:, -1]), 0.0)
        return (block_decay[:, None, None] * running_state + block_state, block_out)
    start_state = jnp.zeros((HEADS, N, P_SIZE), jnp.float32)
    final_state, outputs = lax.scan(advance, start_state, (inputs, gates, writes, read_rows, decays, labels, before))
    return outputs.reshape(JOINED_SIZE, HEADS * P_SIZE)

def attention_part(queries, key_matrix_rows, value_matrix_rows, segment):
    query_group = QUERY_HEAD_COUNT // KEY_VALUE_HEADS
    token_span = (CYCLE + 1) * SEGMENT_SIZE
    error_margin = CYCLE * SEGMENT_SIZE
    scale = 1.0 / math.sqrt(HEAD_WIDTH)
    keys_with_padding = jnp.concatenate([jnp.zeros((error_margin, KEY_VALUE_HEADS * HEAD_WIDTH), jnp.bfloat16), key_matrix_rows])
    values_with_padding = jnp.concatenate([jnp.zeros((error_margin, KEY_VALUE_HEADS * HEAD_WIDTH), jnp.bfloat16), value_matrix_rows])
    padded_segment = jnp.concatenate([jnp.full((error_margin,), -1, jnp.int32), segment]).astype(jnp.int32)
    padded_positions = (jnp.arange(JOINED_SIZE + error_margin) - error_margin).astype(jnp.int32)

    def slab_fn(slab):
        first_entry = (slab * SEGMENT_SIZE).astype(jnp.int32)
        block_of_queries = lax.dynamic_slice_in_dim(queries, first_entry, SEGMENT_SIZE, 0).reshape(SEGMENT_SIZE, KEY_VALUE_HEADS, query_group, HEAD_WIDTH)
        block_of_keys = lax.dynamic_slice_in_dim(keys_with_padding, first_entry, token_span, 0).reshape(token_span, KEY_VALUE_HEADS, HEAD_WIDTH)
        block_of_values = lax.dynamic_slice_in_dim(values_with_padding, first_entry, token_span, 0).reshape(token_span, KEY_VALUE_HEADS, HEAD_WIDTH)
        query_segment = lax.dynamic_slice_in_dim(segment, first_entry, SEGMENT_SIZE, 0)
        query_positions = (first_entry + jnp.arange(SEGMENT_SIZE)).astype(jnp.int32)
        key_segment = lax.dynamic_slice_in_dim(padded_segment, first_entry, token_span, 0)
        key_positions = lax.dynamic_slice_in_dim(padded_positions, first_entry, token_span, 0)
        allowed = (query_segment[:, None] == key_segment[None, :]) & (key_positions[None, :] <= query_positions[:, None])

        def per_head_attend(head):
            query_head = block_of_queries[:, head].astype(jnp.float32)
            key_head = block_of_keys[:, head].astype(jnp.float32)
            value_head = block_of_values[:, head].astype(jnp.float32)
            scores = jnp.einsum('tgd,sd->gts', query_head, key_head) * scale
            masked = jnp.where(allowed[None], scores, -jnp.inf)
            largest = lax.optimization_barrier(jnp.max(masked, axis=2, keepdims=True))
            weights = jnp.where(allowed[None], jnp.exp(masked - largest), 0.0)
            totals = lax.optimization_barrier(jnp.sum(weights, axis=2))
            rounded = lax.optimization_barrier(weights.astype(jnp.bfloat16))
            summed = jnp.einsum('gts,sd->tgd', rounded.astype(jnp.float32), value_head)
            return summed / totals.T[:, :, None]
        output_per_head = lax.map(per_head_attend, jnp.arange(KEY_VALUE_HEADS).astype(jnp.int32))
        return output_per_head.transpose(1, 0, 2, 3).reshape(SEGMENT_SIZE, QUERY_HEAD_COUNT * HEAD_WIDTH).astype(jnp.bfloat16)
    slabs = lax.map(slab_fn, jnp.arange(N_SEQ).astype(jnp.int32))
    return slabs.reshape(JOINED_SIZE, QUERY_HEAD_COUNT * HEAD_WIDTH)

def reference(mixer_input, mixer_gate, state_write, state_read, log_decay, norm_gain, queries, key_matrix_rows, value_matrix_rows, request_blocks):
    positions = jnp.arange(JOINED_SIZE).astype(jnp.int32)
    segment = segment_ids(request_blocks, positions)
    mixer_out = mixer_part(mixer_input, mixer_gate, state_write, state_read, log_decay, norm_gain, segment)
    attention_out = attention_part(queries, key_matrix_rows, value_matrix_rows, segment)
    return (mixer_out, attention_out)
```

```python
import math

import jax
import jax.numpy as jnp
from jax import lax
from jax.experimental import pallas as pl
from jax.experimental.pallas import tpu as pltpu
from jax.sharding import PartitionSpec as P

HEADS = 128
P_SIZE = 128
N = 128
HEAD_WIDTH = 128
BLOCK = 128
EXTRA = 8
F32 = jnp.float32
BF16 = jnp.bfloat16
VMEM = pl.BlockSpec(memory_space=pltpu.VMEM)
SMEM = pl.BlockSpec(memory_space=pltpu.SMEM)
MIB = 1024 * 1024


def request_ends(lengths_ref):
    ends = []
    total = 0
    for r in range(lengths_ref.shape[0]):
        total = total + lengths_ref[r]
        ends.append(total)
    return ends


def starts_request(ends, block):
    found = block == 0
    for end in ends:
        found = found | (block == end)
    return found


def first_block(ends, block):
    first = 0
    for end in ends:
        first = jnp.where(end <= block, end, first)
    return first


def summed_along(log_decay, chosen):
    heads = log_decay.shape[0]
    high = log_decay.astype(BF16)
    rest = log_decay - high.astype(F32)
    middle = rest.astype(BF16)
    low = (rest - middle.astype(F32)).astype(BF16)
    parts = jnp.concatenate([high, middle, low], axis=0)
    sums = jnp.dot(parts, chosen, preferred_element_type=F32)
    return sums[:heads] + sums[heads : 2 * heads] + sums[2 * heads :]


def state_kernel(lengths_ref, input_ref, write_ref, decay_ref, out_ref):
    heads, rows = decay_ref.shape
    place = lax.axis_index("seq")
    ends = request_ends(lengths_ref)
    opens_0 = starts_request(ends, 2 * place)
    opens_1 = starts_request(ends, 2 * place + 1)
    log_decay = decay_ref[...]
    u = lax.broadcasted_iota(jnp.int32, (rows, rows), 0)
    j = lax.broadcasted_iota(jnp.int32, (rows, rows), 1)
    after = summed_along(log_decay, jnp.where(u > j, 1.0, 0.0).astype(BF16))
    total = after[:, :1] + log_decay[:, :1]
    token = lax.broadcasted_iota(jnp.int32, (heads, rows), 1)
    reaching = jnp.where((token < BLOCK) & opens_1, 0.0, jnp.exp(after))
    passing = jnp.where(opens_0 | opens_1, 0.0, jnp.exp(total))
    high = passing.astype(BF16).astype(F32)
    rest = passing - high
    middle = rest.astype(BF16).astype(F32)
    low = rest - middle
    line = lax.broadcasted_iota(jnp.int32, (EXTRA, 128), 0)
    writes = write_ref[...].astype(F32).T
    half = N // 2
    for h in range(heads):
        scaled = (writes * reaching[h : h + 1, :]).astype(BF16)
        state = jnp.dot(
            scaled, input_ref[:, h * P_SIZE : (h + 1) * P_SIZE], preferred_element_type=F32
        )
        tail = jnp.where(
            line == 0,
            high[h : h + 1, :],
            jnp.where(line == 1, middle[h : h + 1, :], jnp.where(line == 2, low[h : h + 1, :], 0.0)),
        )
        for part in range(2):
            out_ref[2 * h + part] = jnp.concatenate(
                [state[part * half : (part + 1) * half], tail], axis=0
            ).astype(BF16)


def scan_kernel(states_ref, out_ref):
    count, rows, _ = out_ref.shape
    entering = jnp.zeros(out_ref.shape[1:], F32)
    for d in range(count):
        out_ref[d] = entering.astype(BF16)
        block = states_ref[d].astype(F32)
        passing = block[rows : rows + 1] + block[rows + 1 : rows + 2] + block[rows + 2 : rows + 3]
        entering = passing * entering + block[:rows]


def within_kernel(
    lengths_ref, input_ref, gate_ref, write_ref, read_ref, decay_ref, within_ref, factor_ref
):
    heads, rows = decay_ref.shape
    place = lax.axis_index("seq")
    ends = request_ends(lengths_ref)
    opens_0 = starts_request(ends, 2 * place)
    opens_1 = starts_request(ends, 2 * place + 1)
    u = lax.broadcasted_iota(jnp.int32, (rows, rows), 0)
    j = lax.broadcasted_iota(jnp.int32, (rows, rows), 1)
    running = summed_along(decay_ref[...], jnp.where(u <= j, 1.0, 0.0).astype(BF16))
    down = running.T
    token = lax.broadcasted_iota(jnp.int32, (rows, heads), 0)
    cut = opens_0 | ((token >= BLOCK) & opens_1)
    entry = jnp.where(cut, 0.0, jnp.exp(down))
    affinity = lax.dot_general(
        read_ref[...], write_ref[...], (((1,), (1,)), ((), ())), preferred_element_type=F32
    )
    seen = (j <= u) & jnp.logical_not((u >= BLOCK) & (j < BLOCK) & opens_1)
    affinity = jnp.where(seen, affinity, 0.0)
    for h in range(heads):
        columns = slice(h * P_SIZE, (h + 1) * P_SIZE)
        column = down[:, h : h + 1]
        line = running[h : h + 1, :]
        top = jnp.exp(jnp.minimum(column[:BLOCK] - line[:, :BLOCK], 0.0)) * affinity[:BLOCK, :BLOCK]
        bottom = jnp.exp(jnp.minimum(column[BLOCK:] - line, 0.0)) * affinity[BLOCK:]
        inputs = input_ref[:, columns]
        gate = gate_ref[:, columns].astype(F32)
        silu = gate / (1.0 + jnp.exp(-gate))
        within_ref[:BLOCK, columns] = silu[:BLOCK] * jnp.dot(
            top.astype(BF16), inputs[:BLOCK], preferred_element_type=F32
        )
        within_ref[BLOCK:, columns] = silu[BLOCK:] * jnp.dot(
            bottom.astype(BF16), inputs, preferred_element_type=F32
        )
        factor_ref[:, columns] = silu * entry[:, h : h + 1]


def mixed_kernel(within_ref, factor_ref, read_ref, entering_ref, gated_ref, squares_ref):
    rows, width = within_ref.shape
    heads = width // P_SIZE
    reads = read_ref[...]
    squares = jnp.zeros((rows, 2 * P_SIZE), F32)
    for h in range(0, heads, 2):
        columns = slice(h * P_SIZE, (h + 2) * P_SIZE)
        pair = jnp.concatenate(
            [
                jnp.concatenate([entering_ref[2 * k], entering_ref[2 * k + 1]], axis=0)
                for k in (h, h + 1)
            ],
            axis=1,
        )
        from_state = jnp.dot(reads, pair, preferred_element_type=F32)
        gated = within_ref[:, columns] + factor_ref[:, columns] * from_state
        gated_ref[:, columns] = gated
        squares = squares + gated * gated
    folded = squares[:, :P_SIZE] + squares[:, P_SIZE:]
    squares_ref[...] = jnp.sum(folded.T, axis=0, keepdims=True)


def scale_kernel(gated_ref, squares_ref, gain_ref, out_ref):
    copies, _, rows = squares_ref.shape
    total = squares_ref[0]
    for k in range(1, copies):
        total = total + squares_ref[k]
    scaling = lax.rsqrt(total / (HEADS * P_SIZE) + 1e-05)
    column = jnp.broadcast_to(scaling, (128, rows)).T[:, :1]
    out_ref[...] = (gated_ref[...] * column * gain_ref[...]).astype(BF16)


def attention_kernel(lengths_ref, query_ref, *refs):
    pair_refs, out_ref = refs[:-1], refs[-1]
    rows, width = query_ref.shape
    place = lax.axis_index("seq")
    ends = request_ends(lengths_ref)
    scale = math.log2(math.e) / math.sqrt(HEAD_WIDTH)
    i = lax.broadcasted_iota(jnp.int32, (BLOCK, BLOCK), 0)
    j = lax.broadcasted_iota(jnp.int32, (BLOCK, BLOCK), 1)
    causal = jnp.where(j <= i, 0.0, -jnp.inf)
    steps = len(pair_refs)
    firsts = [first_block(ends, 2 * place + a) for a in range(2)]
    hidden = [
        [
            [
                jnp.where(2 * (place - step) + part >= firsts[a], 0.0, -jnp.inf)
                for part in range(2)
            ]
            for step in range(steps)
        ]
        for a in range(2)
    ]

    def one(g, _):
        at = pl.ds(pl.multiple_of(g * HEAD_WIDTH, HEAD_WIDTH), HEAD_WIDTH)
        queries = query_ref[:, at]
        scores = [
            lax.dot_general(
                queries, pair[:rows, :], (((1,), (1,)), ((), ())), preferred_element_type=F32
            )
            for pair in pair_refs
        ]
        for a in range(2):
            down = slice(a * BLOCK, (a + 1) * BLOCK)
            tiles = []
            for step in range(steps):
                for part in range(2):
                    if step == 0 and part > a:
                        continue
                    tile = scores[step][down, part * BLOCK : (part + 1) * BLOCK] * scale
                    tile = tile + (causal if step == 0 and part == a else hidden[a][step][part])
                    tiles.append((step, part, tile))
            largest = tiles[0][2]
            for _, _, tile in tiles[1:]:
                largest = jnp.maximum(largest, tile)
            largest = jnp.max(largest, axis=1, keepdims=True)
            weights = [(step, part, jnp.exp2(tile - largest)) for step, part, tile in tiles]
            total = weights[0][2]
            for _, _, weight in weights[1:]:
                total = total + weight
            total = jnp.sum(total, axis=1, keepdims=True)
            summed = jnp.zeros((BLOCK, HEAD_WIDTH), F32)
            for step in range(steps):
                mine = [weight.astype(BF16) for s, _, weight in weights if s == step]
                rounded = jnp.concatenate(mine, axis=1)
                values = pair_refs[step][rows : rows + BLOCK * len(mine), :]
                summed = summed + jnp.dot(rounded, values, preferred_element_type=F32)
            out_ref[down, at] = (summed / total).astype(BF16)
        return 0

    lax.fori_loop(0, width // HEAD_WIDTH, one, 0)


def call(kernel, ins, outs, limit, flops=0, nbytes=0, transcendentals=0, name=None):
    return pl.pallas_call(
        kernel,
        in_specs=ins,
        out_specs=jax.tree.map(lambda _: VMEM, outs),
        out_shape=outs,
        compiler_params=pltpu.CompilerParams(vmem_limit_bytes=limit * MIB),
        cost_estimate=pl.CostEstimate(
            flops=flops, bytes_accessed=nbytes, transcendentals=transcendentals
        ),
        name=name,
    )


def shifted(shard, by):
    count = lax.axis_size("seq")
    return lax.ppermute(shard, "seq", [(i, (i + by) % count) for i in range(count)])


def on_device(
    mixer_input,
    mixer_gate,
    state_write,
    state_read,
    log_decay,
    norm_gain,
    queries,
    key_matrix_rows,
    value_matrix_rows,
    request_blocks,
):
    rows, width = mixer_input.shape
    count = lax.axis_size("seq")
    copies = lax.axis_size("tp")
    part = width // P_SIZE * N // count
    shape = jax.ShapeDtypeStruct

    own_pair = jnp.concatenate([key_matrix_rows, value_matrix_rows], axis=0)
    pairs = [own_pair] + [shifted(own_pair, by) for by in range(1, 5)]

    states = call(
        state_kernel,
        [SMEM, VMEM, VMEM, VMEM],
        shape((count, part + EXTRA, P_SIZE), BF16),
        16,
        flops=2 * rows * width * N,
        nbytes=2 * rows * width,
        name="states",
    )(request_blocks, mixer_input, state_write, log_decay)
    states = lax.all_to_all(states, "seq", 0, 0)

    attention_out = call(
        attention_kernel,
        [SMEM] + [VMEM] * 6,
        shape(queries.shape, BF16),
        24,
        flops=4 * rows * 5 * rows * queries.shape[1],
        nbytes=4 * rows * queries.shape[1],
        transcendentals=8 * rows * 5 * rows,
        name="attention",
    )(request_blocks, queries, *pairs)

    entering = call(
        scan_kernel,
        [VMEM],
        shape((count, part, P_SIZE), BF16),
        16,
        flops=2 * count * part * P_SIZE,
        nbytes=4 * count * part * P_SIZE,
        name="scan",
    )(states)
    entering = lax.all_to_all(entering, "seq", 0, 0)

    wide = shape((rows, width), F32)
    within, factor = call(
        within_kernel,
        [SMEM] + [VMEM] * 5,
        (wide, wide),
        24,
        flops=2 * rows * rows * width,
        nbytes=12 * rows * width,
        transcendentals=3 * rows * width,
        name="within",
    )(request_blocks, mixer_input, mixer_gate, state_write, state_read, log_decay)

    gated, squares = call(
        mixed_kernel,
        [VMEM] * 4,
        (wide, shape((1, rows), F32)),
        24,
        flops=2 * rows * N * width,
        nbytes=12 * rows * width,
        name="mixed",
    )(within, factor, state_read, entering)
    squares = lax.all_to_all(jnp.broadcast_to(squares[None], (copies, 1, rows)), "tp", 0, 0)

    mixer_out = call(
        scale_kernel,
        [VMEM] * 3,
        shape((rows, width), BF16),
        24,
        flops=2 * rows * width,
        nbytes=6 * rows * width,
        name="scaled",
    )(gated, squares, norm_gain[None, :])
    return (mixer_out, attention_out)


def solution(mesh):
    placed = (
        P("seq", "tp"),
        P("seq", "tp"),
        P("seq", None),
        P("seq", None),
        P("tp", "seq"),
        P("tp"),
        P("seq", "tp"),
        P("seq", "tp"),
        P("seq", "tp"),
        P(),
    )
    return jax.shard_map(
        on_device,
        mesh=mesh,
        in_specs=placed,
        out_specs=(P("seq", "tp"), P("seq", "tp")),
        check_vma=False,
    )
```

```python
from functools import partial
import math

import jax
import jax.numpy as jnp
from jax import lax
from jax.experimental import pallas as pl
from jax.experimental.pallas import tpu as pltpu
from jax.sharding import PartitionSpec as P

HEADS = 128
P_SIZE = 128
N = 128
HEAD_WIDTH = 128
BLOCK = 128
EXTRA = 8
F32 = jnp.float32
BF16 = jnp.bfloat16
VMEM = pl.BlockSpec(memory_space=pltpu.VMEM)
HBM = pl.BlockSpec(memory_space=pltpu.HBM)
SMEM = pl.BlockSpec(memory_space=pltpu.SMEM)
MIB = 1024 * 1024
PIECES = 4


def fetch(pairs, sems):
    copies = [
        pltpu.make_async_copy(source, target, sems.at[k]) for k, (source, target) in enumerate(pairs)
    ]
    for copy in copies:
        copy.start()
    return copies


def column_pieces(source, target):
    width = target.shape[1] // PIECES
    columns = [pl.ds(k * width, width) for k in range(PIECES)]
    return [(source.at[:, at], target.at[:, at]) for at in columns]


def request_ends(lengths_ref):
    ends = []
    total = 0
    for r in range(lengths_ref.shape[0]):
        total = total + lengths_ref[r]
        ends.append(total)
    return ends


def starts_request(ends, block):
    found = block == 0
    for end in ends:
        found = found | (block == end)
    return found


def first_block(ends, block):
    first = 0
    for end in ends:
        first = jnp.where(end <= block, end, first)
    return first


def summed_along(log_decay, chosen):
    heads = log_decay.shape[0]
    high = log_decay.astype(BF16)
    rest = log_decay - high.astype(F32)
    middle = rest.astype(BF16)
    low = (rest - middle.astype(F32)).astype(BF16)
    parts = jnp.concatenate([high, middle, low], axis=0)
    sums = jnp.dot(parts, chosen, preferred_element_type=F32)
    return sums[:heads] + sums[heads : 2 * heads] + sums[2 * heads :]


def pair_kernel(key_ref, value_ref, out_ref):
    rows = key_ref.shape[0]
    out_ref[:rows] = key_ref[...]
    out_ref[rows:] = value_ref[...]


def state_kernel(
    lengths_hbm,
    input_hbm,
    write_hbm,
    decay_hbm,
    out_ref,
    lengths_ref,
    input_ref,
    write_ref,
    decay_ref,
    sems,
):
    heads, rows = decay_ref.shape
    copies = fetch(
        [(decay_hbm, decay_ref), (write_hbm, write_ref)]
        + column_pieces(input_hbm, input_ref)
        + [(lengths_hbm, lengths_ref)],
        sems,
    )
    copies[-1].wait()
    copies[0].wait()
    place = lax.axis_index("seq")
    ends = request_ends(lengths_ref)
    opens_0 = starts_request(ends, 2 * place)
    opens_1 = starts_request(ends, 2 * place + 1)
    log_decay = decay_ref[...]
    u = lax.broadcasted_iota(jnp.int32, (rows, rows), 0)
    j = lax.broadcasted_iota(jnp.int32, (rows, rows), 1)
    after = summed_along(log_decay, jnp.where(u > j, 1.0, 0.0).astype(BF16))
    total = after[:, :1] + log_decay[:, :1]
    token = lax.broadcasted_iota(jnp.int32, (heads, rows), 1)
    reaching = jnp.where((token < BLOCK) & opens_1, 0.0, jnp.exp(after))
    passing = jnp.where(opens_0 | opens_1, 0.0, jnp.exp(total))
    high = passing.astype(BF16).astype(F32)
    rest = passing - high
    middle = rest.astype(BF16).astype(F32)
    low = rest - middle
    line = lax.broadcasted_iota(jnp.int32, (EXTRA, 128), 0)
    copies[1].wait()
    writes = write_ref[...].astype(F32).T
    half = N // 2
    for h in range(heads):
        if h % (heads // PIECES) == 0:
            copies[2 + h // (heads // PIECES)].wait()
        scaled = (writes * reaching[h : h + 1, :]).astype(BF16)
        state = jnp.dot(
            scaled, input_ref[:, h * P_SIZE : (h + 1) * P_SIZE], preferred_element_type=F32
        )
        tail = jnp.where(
            line == 0,
            high[h : h + 1, :],
            jnp.where(line == 1, middle[h : h + 1, :], jnp.where(line == 2, low[h : h + 1, :], 0.0)),
        )
        for part in range(2):
            out_ref[2 * h + part] = jnp.concatenate(
                [state[part * half : (part + 1) * half], tail], axis=0
            ).astype(BF16)


def scan_kernel(states_ref, out_ref):
    count, rows, _ = out_ref.shape
    entering = jnp.zeros(out_ref.shape[1:], F32)
    for d in range(count):
        out_ref[d] = entering.astype(BF16)
        block = states_ref[d].astype(F32)
        passing = block[rows : rows + 1] + block[rows + 1 : rows + 2] + block[rows + 2 : rows + 3]
        entering = passing * entering + block[:rows]


def within_kernel(
    lengths_ref, input_ref, gate_ref, write_ref, read_ref, decay_ref, out_ref
):
    heads, rows = decay_ref.shape
    place = lax.axis_index("seq")
    ends = request_ends(lengths_ref)
    opens_0 = starts_request(ends, 2 * place)
    opens_1 = starts_request(ends, 2 * place + 1)
    u = lax.broadcasted_iota(jnp.int32, (rows, rows), 0)
    j = lax.broadcasted_iota(jnp.int32, (rows, rows), 1)
    running = summed_along(decay_ref[...], jnp.where(u <= j, 1.0, 0.0).astype(BF16))
    down = running.T
    token = lax.broadcasted_iota(jnp.int32, (rows, heads), 0)
    cut = opens_0 | ((token >= BLOCK) & opens_1)
    entry = jnp.where(cut, 0.0, jnp.exp(down))
    affinity = lax.dot_general(
        read_ref[...], write_ref[...], (((1,), (1,)), ((), ())), preferred_element_type=F32
    )
    seen = (j <= u) & jnp.logical_not((u >= BLOCK) & (j < BLOCK) & opens_1)
    affinity = jnp.where(seen, affinity, 0.0)
    for h in range(heads):
        columns = slice(h * P_SIZE, (h + 1) * P_SIZE)
        column = down[:, h : h + 1]
        line = running[h : h + 1, :]
        top = jnp.exp(jnp.minimum(column[:BLOCK] - line[:, :BLOCK], 0.0)) * affinity[:BLOCK, :BLOCK]
        bottom = jnp.exp(jnp.minimum(column[BLOCK:] - line, 0.0)) * affinity[BLOCK:]
        inputs = input_ref[:, columns]
        gate = gate_ref[:, columns].astype(F32)
        silu = gate / (1.0 + jnp.exp(-gate))
        out_ref[0, :BLOCK, columns] = (
            silu[:BLOCK]
            * jnp.dot(top.astype(BF16), inputs[:BLOCK], preferred_element_type=F32)
        ).astype(BF16)
        out_ref[0, BLOCK:, columns] = (
            silu[BLOCK:] * jnp.dot(bottom.astype(BF16), inputs, preferred_element_type=F32)
        ).astype(BF16)
        out_ref[1, :, columns] = (silu * entry[:, h : h + 1]).astype(BF16)


def mixed_kernel(within_ref, read_ref, entering_ref, gated_ref, squares_ref):
    _, rows, width = within_ref.shape
    heads = width // P_SIZE
    reads = read_ref[...]
    squares = jnp.zeros((rows, 2 * P_SIZE), F32)
    for h in range(0, heads, 2):
        columns = slice(h * P_SIZE, (h + 2) * P_SIZE)
        pair = jnp.concatenate(
            [
                jnp.concatenate([entering_ref[2 * k], entering_ref[2 * k + 1]], axis=0)
                for k in (h, h + 1)
            ],
            axis=1,
        )
        from_state = jnp.dot(reads, pair, preferred_element_type=F32)
        within = within_ref[0, :, columns].astype(F32)
        gated = within + within_ref[1, :, columns].astype(F32) * from_state
        gated_ref[:, columns] = gated
        squares = squares + gated * gated
    folded = squares[:, :P_SIZE] + squares[:, P_SIZE:]
    row = jnp.sum(folded.T, axis=0, keepdims=True)
    for k in range(squares_ref.shape[0]):
        squares_ref[k] = row


def scale_kernel(gated_ref, squares_ref, gain_ref, out_hbm, out_ref, sems):
    copies, _, rows = squares_ref.shape
    total = squares_ref[0]
    for k in range(1, copies):
        total = total + squares_ref[k]
    scaling = lax.rsqrt(total / (HEADS * P_SIZE) + 1e-05)
    column = jnp.broadcast_to(scaling, (128, rows)).T[:, :1]
    width = out_ref.shape[1] // PIECES
    started = []
    for k, (target, source) in enumerate(column_pieces(out_hbm, out_ref)):
        at = slice(k * width, (k + 1) * width)
        out_ref[:, at] = (gated_ref[:, at].astype(F32) * column * gain_ref[:, at]).astype(BF16)
        copy = pltpu.make_async_copy(source, target, sems.at[k])
        copy.start()
        started.append(copy)
    for copy in started:
        copy.wait()


def attention_kernel(steps, opens, closes, lengths_ref, query_ref, *refs):
    pair_refs, refs = refs[: len(steps)], refs[len(steps) :]
    if not opens:
        summed_in_ref, kept_in_ref, *refs = refs
    rows, width = query_ref.shape
    heads = width // HEAD_WIDTH
    place = lax.axis_index("seq")
    ends = request_ends(lengths_ref)
    scale = math.log2(math.e) / math.sqrt(HEAD_WIDTH)
    i = lax.broadcasted_iota(jnp.int32, (BLOCK, BLOCK), 0)
    j = lax.broadcasted_iota(jnp.int32, (BLOCK, BLOCK), 1)
    causal = jnp.where(j <= i, 0.0, -jnp.inf)
    firsts = [first_block(ends, 2 * place + a) for a in range(2)]

    def hidden(a, step, part):
        return jnp.where(2 * (place - step) + part >= firsts[a], 0.0, -jnp.inf)

    for g in range(heads):
        at = slice(g * HEAD_WIDTH, (g + 1) * HEAD_WIDTH)
        queries = query_ref[:, at]
        scores = [
            lax.dot_general(
                queries, pair[:rows, :], (((1,), (1,)), ((), ())), preferred_element_type=F32
            )
            for pair in pair_refs
        ]
        for a in range(2):
            down = slice(a * BLOCK, (a + 1) * BLOCK)
            tiles = []
            for k, step in enumerate(steps):
                for part in range(2):
                    if step == 0 and part > a:
                        continue
                    tile = scores[k][down, part * BLOCK : (part + 1) * BLOCK] * scale
                    tile = tile + (causal if step == 0 and part == a else hidden(a, step, part))
                    tiles.append((k, tile))
            largest = tiles[0][1]
            for _, tile in tiles[1:]:
                largest = jnp.maximum(largest, tile)
            largest = jnp.max(largest, axis=1, keepdims=True)
            if not opens:
                before = kept_in_ref[down, g : g + 1]
                largest = jnp.maximum(largest, before)
            weights = [(k, jnp.exp2(tile - largest)) for k, tile in tiles]
            total = weights[0][1]
            for _, weight in weights[1:]:
                total = total + weight
            total = jnp.sum(total, axis=1, keepdims=True)
            summed = None
            if not opens:
                kept = jnp.exp2(before - largest)
                total = total + kept * kept_in_ref[down, heads + g : heads + g + 1]
                summed = kept * summed_in_ref[down, at]
            for k in range(len(steps)):
                mine = [weight.astype(BF16) for m, weight in weights if m == k]
                values = pair_refs[k][rows : rows + BLOCK * len(mine), :]
                term = jnp.dot(
                    jnp.concatenate(mine, axis=1), values, preferred_element_type=F32
                )
                summed = term if summed is None else summed + term
            if closes:
                refs[0][down, at] = (summed / total).astype(BF16)
            else:
                refs[0][down, at] = summed
                refs[1][down, g : g + 1] = largest
                refs[1][down, heads + g : heads + g + 1] = total


def call(
    kernel, ins, outs, limit, flops=0, nbytes=0, transcendentals=0, name=None, places=None, scratch=()
):
    return pl.pallas_call(
        kernel,
        in_specs=ins,
        out_specs=places or jax.tree.map(lambda _: VMEM, outs),
        out_shape=outs,
        scratch_shapes=list(scratch),
        compiler_params=pltpu.CompilerParams(vmem_limit_bytes=limit * MIB),
        cost_estimate=pl.CostEstimate(
            flops=flops, bytes_accessed=nbytes, transcendentals=transcendentals
        ),
        name=name,
    )


def shifted(shard, by):
    count = lax.axis_size("seq")
    return lax.ppermute(shard, "seq", [(i, (i + by) % count) for i in range(count)])


def on_device(
    mixer_input,
    mixer_gate,
    state_write,
    state_read,
    log_decay,
    norm_gain,
    queries,
    key_matrix_rows,
    value_matrix_rows,
    request_blocks,
):
    rows, width = mixer_input.shape
    count = lax.axis_size("seq")
    copies = lax.axis_size("tp")
    part = width // P_SIZE * N // count
    shape = jax.ShapeDtypeStruct

    lengths = pltpu.SMEM(request_blocks.shape, jnp.int32)
    whole = pltpu.VMEM((rows, width), BF16)
    own_pair = call(
        pair_kernel,
        [VMEM] * 2,
        shape((2 * rows, HEAD_WIDTH), BF16),
        4,
        nbytes=4 * rows * HEAD_WIDTH,
        name="pair",
    )(key_matrix_rows, value_matrix_rows)
    behind_1 = shifted(own_pair, 1)
    behind_2 = shifted(own_pair, 2)

    states = call(
        state_kernel,
        [HBM] * 4,
        shape((count, part + EXTRA, P_SIZE), BF16),
        60,
        flops=2 * rows * width * N,
        nbytes=2 * rows * width,
        name="states",
        scratch=[
            lengths,
            whole,
            pltpu.VMEM((rows, N), BF16),
            pltpu.VMEM(log_decay.shape, F32),
            pltpu.SemaphoreType.DMA((3 + PIECES,)),
        ],
    )(request_blocks, mixer_input, state_write, log_decay)
    states = lax.all_to_all(states, "seq", 0, 0)

    summed, kept = call(
        partial(attention_kernel, (0, 1, 2), True, False),
        [SMEM] + [VMEM] * 4,
        (shape(queries.shape, F32), shape((rows, 128), F32)),
        16,
        flops=64 * rows * 3 * rows * queries.shape[1],
        nbytes=4 * rows * queries.shape[1],
        transcendentals=8 * rows * 3 * rows,
        name="attention_near",
    )(request_blocks, queries, own_pair, behind_1, behind_2)
    states, summed, kept = lax.optimization_barrier((states, summed, kept))

    entering = call(
        scan_kernel,
        [VMEM],
        shape((count, part, P_SIZE), BF16),
        8,
        flops=2 * count * part * P_SIZE,
        nbytes=4 * count * part * P_SIZE,
        name="scan",
    )(states)
    entering = lax.all_to_all(entering, "seq", 0, 0)

    behind_3 = shifted(behind_2, 1)
    behind_4 = shifted(behind_2, 2)
    within = call(
        within_kernel,
        [SMEM] + [VMEM] * 5,
        shape((2, rows, width), BF16),
        8,
        flops=2 * rows * rows * width,
        nbytes=12 * rows * width,
        transcendentals=3 * rows * width,
        name="within",
    )(request_blocks, mixer_input, mixer_gate, state_write, state_read, log_decay)

    attention_out = call(
        partial(attention_kernel, (3, 4), False, True),
        [SMEM] + [VMEM] * 5,
        shape(queries.shape, BF16),
        16,
        flops=64 * rows * 3 * rows * queries.shape[1],
        nbytes=8 * rows * queries.shape[1],
        transcendentals=8 * rows * 2 * rows,
        name="attention_far",
    )(request_blocks, queries, behind_3, behind_4, summed, kept)
    entering, attention_out = lax.optimization_barrier((entering, attention_out))

    gated, squares = call(
        mixed_kernel,
        [VMEM] * 3,
        (shape((rows, width), F32), shape((copies, 1, rows), F32)),
        8,
        flops=2 * rows * N * width,
        nbytes=12 * rows * width,
        name="mixed",
    )(within, state_read, entering)
    squares = lax.all_to_all(squares, "tp", 0, 0)

    mixer_out = call(
        scale_kernel,
        [VMEM] * 3,
        shape((rows, width), BF16),
        8,
        flops=2 * rows * width,
        nbytes=6 * rows * width,
        name="scaled",
        places=HBM,
        scratch=[whole, pltpu.SemaphoreType.DMA((PIECES,))],
    )(gated, squares, norm_gain[None, :])
    return (mixer_out, attention_out)


def solution(mesh):
    placed = (
        P("seq", "tp"),
        P("seq", "tp"),
        P("seq", None),
        P("seq", None),
        P("tp", "seq"),
        P("tp"),
        P("seq", "tp"),
        P("seq", "tp"),
        P("seq", "tp"),
        P(),
    )
    return jax.shard_map(
        on_device,
        mesh=mesh,
        in_specs=placed,
        out_specs=(P("seq", "tp"), P("seq", "tp")),
        check_vma=False,
    )
```

```python
from functools import partial
import math

import jax
import jax.numpy as jnp
from jax import lax
from jax.experimental import pallas as pl
from jax.experimental.pallas import tpu as pltpu
from jax.sharding import PartitionSpec as P

HEADS = 128
P_SIZE = 128
N = 128
HEAD_WIDTH = 128
BLOCK = 128
EXTRA = 8
F32 = jnp.float32
BF16 = jnp.bfloat16
VMEM = pl.BlockSpec(memory_space=pltpu.VMEM)
HBM = pl.BlockSpec(memory_space=pltpu.HBM)
SMEM = pl.BlockSpec(memory_space=pltpu.SMEM)
MIB = 1024 * 1024
PIECES = 4


def fetch(pairs, sems):
    copies = [
        pltpu.make_async_copy(source, target, sems.at[k]) for k, (source, target) in enumerate(pairs)
    ]
    for copy in copies:
        copy.start()
    return copies


def column_pieces(source, target):
    width = target.shape[1] // PIECES
    columns = [pl.ds(k * width, width) for k in range(PIECES)]
    return [(source.at[:, at], target.at[:, at]) for at in columns]


def request_ends(lengths_ref):
    ends = []
    total = 0
    for r in range(lengths_ref.shape[0]):
        total = total + lengths_ref[r]
        ends.append(total)
    return ends


def starts_request(ends, block):
    found = block == 0
    for end in ends:
        found = found | (block == end)
    return found


def first_block(ends, block):
    first = 0
    for end in ends:
        first = jnp.where(end <= block, end, first)
    return first


def summed_along(log_decay, chosen):
    heads = log_decay.shape[0]
    high = log_decay.astype(BF16)
    rest = log_decay - high.astype(F32)
    middle = rest.astype(BF16)
    low = (rest - middle.astype(F32)).astype(BF16)
    parts = jnp.concatenate([high, middle, low], axis=0)
    sums = jnp.dot(parts, chosen, preferred_element_type=F32)
    return sums[:heads] + sums[heads : 2 * heads] + sums[2 * heads :]


def state_kernel(
    lengths_hbm,
    input_hbm,
    write_hbm,
    decay_hbm,
    key_hbm,
    value_hbm,
    out_hbm,
    pair_hbm,
    out_ref,
    lengths_ref,
    input_ref,
    write_ref,
    decay_ref,
    pair_ref,
    sems,
    pair_sems,
    pair_out_sem,
    out_sems,
):
    heads, rows = decay_ref.shape
    copies = fetch(
        [(decay_hbm, decay_ref), (write_hbm, write_ref)]
        + column_pieces(input_hbm, input_ref)
        + [(lengths_hbm, lengths_ref)],
        sems,
    )
    keys = fetch(
        [(key_hbm, pair_ref.at[pl.ds(0, rows)]), (value_hbm, pair_ref.at[pl.ds(rows, rows)])],
        pair_sems,
    )
    copies[-1].wait()
    copies[0].wait()
    place = lax.axis_index("seq")
    ends = request_ends(lengths_ref)
    opens_0 = starts_request(ends, 2 * place)
    opens_1 = starts_request(ends, 2 * place + 1)
    log_decay = decay_ref[...]
    u = lax.broadcasted_iota(jnp.int32, (rows, rows), 0)
    j = lax.broadcasted_iota(jnp.int32, (rows, rows), 1)
    after = summed_along(log_decay, jnp.where(u > j, 1.0, 0.0).astype(BF16))
    total = after[:, :1] + log_decay[:, :1]
    token = lax.broadcasted_iota(jnp.int32, (heads, rows), 1)
    reaching = jnp.where((token < BLOCK) & opens_1, 0.0, jnp.exp(after))
    passing = jnp.where(opens_0 | opens_1, 0.0, jnp.exp(total))
    high = passing.astype(BF16).astype(F32)
    rest = passing - high
    middle = rest.astype(BF16).astype(F32)
    low = rest - middle
    line = lax.broadcasted_iota(jnp.int32, (EXTRA, 128), 0)
    for copy in keys:
        copy.wait()
    pair_out = pltpu.make_async_copy(pair_ref, pair_hbm, pair_out_sem)
    pair_out.start()
    copies[1].wait()
    writes = write_ref[...].astype(F32).T
    half = N // 2
    share = out_ref.shape[0] // PIECES
    started = [pair_out]
    for h in range(heads):
        if h % (heads // PIECES) == 0:
            copies[2 + h // (heads // PIECES)].wait()
        scaled = (writes * reaching[h : h + 1, :]).astype(BF16)
        state = jnp.dot(
            scaled, input_ref[:, h * P_SIZE : (h + 1) * P_SIZE], preferred_element_type=F32
        )
        tail = jnp.where(
            line == 0,
            high[h : h + 1, :],
            jnp.where(line == 1, middle[h : h + 1, :], jnp.where(line == 2, low[h : h + 1, :], 0.0)),
        )
        for part in range(2):
            out_ref[2 * h + part] = jnp.concatenate(
                [state[part * half : (part + 1) * half], tail], axis=0
            ).astype(BF16)
        if (h + 1) % (heads // PIECES) == 0:
            k = h // (heads // PIECES)
            at = pl.ds(k * share, share)
            copy = pltpu.make_async_copy(out_ref.at[at], out_hbm.at[at], out_sems.at[k])
            copy.start()
            started.append(copy)
    for copy in started:
        copy.wait()


def scan_kernel(states_ref, out_ref):
    count, rows, _ = out_ref.shape
    entering = jnp.zeros(out_ref.shape[1:], F32)
    for d in range(count):
        out_ref[d] = entering.astype(BF16)
        block = states_ref[d].astype(F32)
        passing = block[rows : rows + 1] + block[rows + 1 : rows + 2] + block[rows + 2 : rows + 3]
        entering = passing * entering + block[:rows]


def within_kernel(
    lengths_hbm,
    input_hbm,
    gate_hbm,
    write_hbm,
    read_hbm,
    decay_hbm,
    out_ref,
    lengths_ref,
    input_ref,
    gate_ref,
    write_ref,
    read_ref,
    decay_ref,
    sems,
):
    heads, rows = decay_ref.shape
    copies = fetch(
        [
            (lengths_hbm, lengths_ref),
            (decay_hbm, decay_ref),
            (write_hbm, write_ref),
            (read_hbm, read_ref),
        ]
        + column_pieces(input_hbm, input_ref)
        + column_pieces(gate_hbm, gate_ref),
        sems,
    )
    for copy in copies[:4]:
        copy.wait()
    place = lax.axis_index("seq")
    ends = request_ends(lengths_ref)
    opens_0 = starts_request(ends, 2 * place)
    opens_1 = starts_request(ends, 2 * place + 1)
    u = lax.broadcasted_iota(jnp.int32, (rows, rows), 0)
    j = lax.broadcasted_iota(jnp.int32, (rows, rows), 1)
    running = summed_along(decay_ref[...], jnp.where(u <= j, 1.0, 0.0).astype(BF16))
    down = running.T
    token = lax.broadcasted_iota(jnp.int32, (rows, heads), 0)
    cut = opens_0 | ((token >= BLOCK) & opens_1)
    entry = jnp.where(cut, 0.0, jnp.exp(down))
    affinity = lax.dot_general(
        read_ref[...], write_ref[...], (((1,), (1,)), ((), ())), preferred_element_type=F32
    )
    seen = (j <= u) & jnp.logical_not((u >= BLOCK) & (j < BLOCK) & opens_1)
    affinity = jnp.where(seen, affinity, 0.0)
    for h in range(heads):
        if h % (heads // PIECES) == 0:
            copies[4 + h // (heads // PIECES)].wait()
            copies[4 + PIECES + h // (heads // PIECES)].wait()
        columns = slice(h * P_SIZE, (h + 1) * P_SIZE)
        column = down[:, h : h + 1]
        line = running[h : h + 1, :]
        top = jnp.exp(jnp.minimum(column[:BLOCK] - line[:, :BLOCK], 0.0)) * affinity[:BLOCK, :BLOCK]
        bottom = jnp.exp(jnp.minimum(column[BLOCK:] - line, 0.0)) * affinity[BLOCK:]
        inputs = input_ref[:, columns]
        gate = gate_ref[:, columns].astype(F32)
        silu = gate / (1.0 + jnp.exp(-gate))
        out_ref[0, :BLOCK, columns] = (
            silu[:BLOCK]
            * jnp.dot(top.astype(BF16), inputs[:BLOCK], preferred_element_type=F32)
        ).astype(BF16)
        out_ref[0, BLOCK:, columns] = (
            silu[BLOCK:] * jnp.dot(bottom.astype(BF16), inputs, preferred_element_type=F32)
        ).astype(BF16)
        out_ref[1, :, columns] = (silu * entry[:, h : h + 1]).astype(BF16)


def mixed_kernel(within_ref, read_ref, entering_ref, gated_ref, squares_ref):
    _, rows, width = within_ref.shape
    heads = width // P_SIZE
    reads = read_ref[...]
    squares = jnp.zeros((rows, 2 * P_SIZE), F32)
    for h in range(0, heads, 2):
        columns = slice(h * P_SIZE, (h + 2) * P_SIZE)
        pair = jnp.concatenate(
            [
                jnp.concatenate([entering_ref[2 * k], entering_ref[2 * k + 1]], axis=0)
                for k in (h, h + 1)
            ],
            axis=1,
        )
        from_state = jnp.dot(reads, pair, preferred_element_type=F32)
        within = within_ref[0, :, columns].astype(F32)
        gated = within + within_ref[1, :, columns].astype(F32) * from_state
        gated_ref[:, columns] = gated
        squares = squares + gated * gated
    folded = squares[:, :P_SIZE] + squares[:, P_SIZE:]
    row = jnp.sum(folded.T, axis=0, keepdims=True)
    for k in range(squares_ref.shape[0]):
        squares_ref[k] = row


def scale_kernel(gated_ref, squares_ref, gain_ref, out_hbm, out_ref, sems):
    copies, _, rows = squares_ref.shape
    total = squares_ref[0]
    for k in range(1, copies):
        total = total + squares_ref[k]
    scaling = lax.rsqrt(total / (HEADS * P_SIZE) + 1e-05)
    column = jnp.broadcast_to(scaling, (128, rows)).T[:, :1]
    width = out_ref.shape[1] // PIECES
    started = []
    for k, (target, source) in enumerate(column_pieces(out_hbm, out_ref)):
        at = slice(k * width, (k + 1) * width)
        out_ref[:, at] = (gated_ref[:, at].astype(F32) * column * gain_ref[:, at]).astype(BF16)
        copy = pltpu.make_async_copy(source, target, sems.at[k])
        copy.start()
        started.append(copy)
    for copy in started:
        copy.wait()


def attention_kernel(steps, opens, closes, *refs):
    ins = 2 + len(steps) + (0 if opens else 2)
    outs = 1 if closes else 2
    sources, targets, refs = refs[:ins], refs[ins : ins + outs], refs[ins + outs :]
    held, results, sems, out_sems = refs[:ins], refs[ins : ins + outs], refs[-2], refs[-1]
    lengths_ref, query_ref = held[:2]
    pair_refs = held[2 : 2 + len(steps)]
    if not opens:
        summed_in_ref, kept_in_ref = held[-2:]
    for copy in fetch(list(zip(sources, held)), sems):
        copy.wait()
    started = []
    rows, width = query_ref.shape
    heads = width // HEAD_WIDTH
    place = lax.axis_index("seq")
    ends = request_ends(lengths_ref)
    scale = math.log2(math.e) / math.sqrt(HEAD_WIDTH)
    i = lax.broadcasted_iota(jnp.int32, (BLOCK, BLOCK), 0)
    j = lax.broadcasted_iota(jnp.int32, (BLOCK, BLOCK), 1)
    causal = jnp.where(j <= i, 0.0, -jnp.inf)
    firsts = [first_block(ends, 2 * place + a) for a in range(2)]

    def hidden(a, step, part):
        return jnp.where(2 * (place - step) + part >= firsts[a], 0.0, -jnp.inf)

    for g in range(heads):
        at = slice(g * HEAD_WIDTH, (g + 1) * HEAD_WIDTH)
        queries = query_ref[:, at]
        scores = [
            lax.dot_general(
                queries, pair[:rows, :], (((1,), (1,)), ((), ())), preferred_element_type=F32
            )
            for pair in pair_refs
        ]
        for a in range(2):
            down = slice(a * BLOCK, (a + 1) * BLOCK)
            tiles = []
            for k, step in enumerate(steps):
                for part in range(2):
                    if step == 0 and part > a:
                        continue
                    tile = scores[k][down, part * BLOCK : (part + 1) * BLOCK] * scale
                    tile = tile + (causal if step == 0 and part == a else hidden(a, step, part))
                    tiles.append((k, tile))
            largest = tiles[0][1]
            for _, tile in tiles[1:]:
                largest = jnp.maximum(largest, tile)
            largest = jnp.max(largest, axis=1, keepdims=True)
            if not opens:
                before = kept_in_ref[down, g : g + 1]
                largest = jnp.maximum(largest, before)
            weights = [(k, jnp.exp2(tile - largest)) for k, tile in tiles]
            total = weights[0][1]
            for _, weight in weights[1:]:
                total = total + weight
            total = jnp.sum(total, axis=1, keepdims=True)
            summed = None
            if not opens:
                kept = jnp.exp2(before - largest)
                total = total + kept * kept_in_ref[down, heads + g : heads + g + 1]
                summed = kept * summed_in_ref[down, at]
            for k in range(len(steps)):
                mine = [weight.astype(BF16) for m, weight in weights if m == k]
                values = pair_refs[k][rows : rows + BLOCK * len(mine), :]
                term = jnp.dot(
                    jnp.concatenate(mine, axis=1), values, preferred_element_type=F32
                )
                summed = term if summed is None else summed + term
            if closes:
                results[0][down, at] = (summed / total).astype(BF16)
            else:
                results[0][down, at] = summed
                results[1][down, g : g + 1] = largest
                results[1][down, heads + g : heads + g + 1] = total
        columns = pl.ds(g * HEAD_WIDTH, HEAD_WIDTH)
        copy = pltpu.make_async_copy(
            results[0].at[:, columns], targets[0].at[:, columns], out_sems.at[g]
        )
        copy.start()
        started.append(copy)
    if not closes:
        copy = pltpu.make_async_copy(results[1], targets[1], out_sems.at[heads])
        copy.start()
        started.append(copy)
    for copy in started:
        copy.wait()


def call(
    kernel, ins, outs, limit, flops=0, nbytes=0, transcendentals=0, name=None, places=None, scratch=()
):
    return pl.pallas_call(
        kernel,
        in_specs=ins,
        out_specs=places or jax.tree.map(lambda _: VMEM, outs),
        out_shape=outs,
        scratch_shapes=list(scratch),
        compiler_params=pltpu.CompilerParams(vmem_limit_bytes=limit * MIB),
        cost_estimate=pl.CostEstimate(
            flops=flops, bytes_accessed=nbytes, transcendentals=transcendentals
        ),
        name=name,
    )


def shifted(shard, by):
    count = lax.axis_size("seq")
    return lax.ppermute(shard, "seq", [(i, (i + by) % count) for i in range(count)])


def on_device(
    mixer_input,
    mixer_gate,
    state_write,
    state_read,
    log_decay,
    norm_gain,
    queries,
    key_matrix_rows,
    value_matrix_rows,
    request_blocks,
):
    rows, width = mixer_input.shape
    count = lax.axis_size("seq")
    copies = lax.axis_size("tp")
    part = width // P_SIZE * N // count
    shape = jax.ShapeDtypeStruct

    lengths = pltpu.SMEM(request_blocks.shape, jnp.int32)
    whole = pltpu.VMEM((rows, width), BF16)
    states, own_pair = call(
        state_kernel,
        [HBM] * 6,
        (
            shape((count, part + EXTRA, P_SIZE), BF16),
            shape((2 * rows, HEAD_WIDTH), BF16),
        ),
        60,
        flops=2 * rows * width * N,
        nbytes=2 * rows * width,
        name="states",
        places=(HBM, HBM),
        scratch=[
            pltpu.VMEM((count, part + EXTRA, P_SIZE), BF16),
            lengths,
            whole,
            pltpu.VMEM((rows, N), BF16),
            pltpu.VMEM(log_decay.shape, F32),
            pltpu.VMEM((2 * rows, HEAD_WIDTH), BF16),
            pltpu.SemaphoreType.DMA((3 + PIECES,)),
            pltpu.SemaphoreType.DMA((2,)),
            pltpu.SemaphoreType.DMA,
            pltpu.SemaphoreType.DMA((PIECES,)),
        ],
    )(request_blocks, mixer_input, state_write, log_decay, key_matrix_rows, value_matrix_rows)
    behind_1 = shifted(own_pair, 1)
    behind_2 = shifted(own_pair, 2)
    states = lax.all_to_all(states, "seq", 0, 0)

    pair = pltpu.VMEM(own_pair.shape, BF16)
    query = pltpu.VMEM(queries.shape, BF16)
    partly = [pltpu.VMEM(queries.shape, F32), pltpu.VMEM((rows, 128), F32)]
    sums = queries.shape[1] // HEAD_WIDTH + 1
    summed, kept = call(
        partial(attention_kernel, (0, 1, 2), True, False),
        [HBM] * 5,
        (shape(queries.shape, F32), shape((rows, 128), F32)),
        60,
        flops=64 * rows * 3 * rows * queries.shape[1],
        nbytes=4 * rows * queries.shape[1],
        transcendentals=8 * rows * 3 * rows,
        name="attention_near",
        places=(HBM, HBM),
        scratch=[lengths, query, pair, pair, pair]
        + partly
        + [pltpu.SemaphoreType.DMA((5,)), pltpu.SemaphoreType.DMA((sums,))],
    )(request_blocks, queries, own_pair, behind_1, behind_2)
    states, summed, kept = lax.optimization_barrier((states, summed, kept))

    entering = call(
        scan_kernel,
        [VMEM],
        shape((count, part, P_SIZE), BF16),
        8,
        flops=2 * count * part * P_SIZE,
        nbytes=4 * count * part * P_SIZE,
        name="scan",
    )(states)
    entering = lax.all_to_all(entering, "seq", 0, 0)

    behind_3 = shifted(behind_2, 1)
    behind_4 = shifted(behind_2, 2)
    within = call(
        within_kernel,
        [HBM] * 6,
        shape((2, rows, width), BF16),
        60,
        flops=2 * rows * rows * width,
        nbytes=12 * rows * width,
        transcendentals=3 * rows * width,
        name="within",
        scratch=[
            lengths,
            whole,
            whole,
            pltpu.VMEM((rows, N), BF16),
            pltpu.VMEM((rows, N), BF16),
            pltpu.VMEM(log_decay.shape, F32),
            pltpu.SemaphoreType.DMA((4 + 2 * PIECES,)),
        ],
    )(request_blocks, mixer_input, mixer_gate, state_write, state_read, log_decay)

    attention_out = call(
        partial(attention_kernel, (3, 4), False, True),
        [HBM] * 6,
        shape(queries.shape, BF16),
        60,
        flops=64 * rows * 3 * rows * queries.shape[1],
        nbytes=8 * rows * queries.shape[1],
        transcendentals=8 * rows * 2 * rows,
        name="attention_far",
        places=HBM,
        scratch=[lengths, query, pair, pair]
        + partly
        + [query, pltpu.SemaphoreType.DMA((6,)), pltpu.SemaphoreType.DMA((sums,))],
    )(request_blocks, queries, behind_3, behind_4, summed, kept)
    entering, attention_out = lax.optimization_barrier((entering, attention_out))

    gated, squares = call(
        mixed_kernel,
        [VMEM] * 3,
        (shape((rows, width), F32), shape((copies, 1, rows), F32)),
        8,
        flops=2 * rows * N * width,
        nbytes=12 * rows * width,
        name="mixed",
    )(within, state_read, entering)
    squares = lax.all_to_all(squares, "tp", 0, 0)

    mixer_out = call(
        scale_kernel,
        [VMEM] * 3,
        shape((rows, width), BF16),
        8,
        flops=2 * rows * width,
        nbytes=6 * rows * width,
        name="scaled",
        places=HBM,
        scratch=[whole, pltpu.SemaphoreType.DMA((PIECES,))],
    )(gated, squares, norm_gain[None, :])
    return (mixer_out, attention_out)


def solution(mesh):
    placed = (
        P("seq", "tp"),
        P("seq", "tp"),
        P("seq", None),
        P("seq", None),
        P("tp", "seq"),
        P("tp"),
        P("seq", "tp"),
        P("seq", "tp"),
        P("seq", "tp"),
        P(),
    )
    return jax.shard_map(
        on_device,
        mesh=mesh,
        in_specs=placed,
        out_specs=(P("seq", "tp"), P("seq", "tp")),
        check_vma=False,
    )
```

```python
from functools import partial
import math

import jax
import jax.numpy as jnp
from jax import lax
from jax.experimental import pallas as pl
from jax.experimental.pallas import tpu as pltpu
from jax.sharding import PartitionSpec as P

HEADS = 128
P_SIZE = 128
N = 128
HEAD_WIDTH = 128
BLOCK = 128
EXTRA = 8
F32 = jnp.float32
BF16 = jnp.bfloat16
VMEM = pl.BlockSpec(memory_space=pltpu.VMEM)
HBM = pl.BlockSpec(memory_space=pltpu.HBM)
SMEM = pl.BlockSpec(memory_space=pltpu.SMEM)
MIB = 1024 * 1024
PIECES = 4


def fetch(pairs, sems):
    copies = [
        pltpu.make_async_copy(source, target, sems.at[k]) for k, (source, target) in enumerate(pairs)
    ]
    for copy in copies:
        copy.start()
    return copies


def column_pieces(source, target):
    width = target.shape[1] // PIECES
    columns = [pl.ds(k * width, width) for k in range(PIECES)]
    return [(source.at[:, at], target.at[:, at]) for at in columns]


def request_ends(lengths_ref):
    ends = []
    total = 0
    for r in range(lengths_ref.shape[0]):
        total = total + lengths_ref[r]
        ends.append(total)
    return ends


def starts_request(ends, block):
    found = block == 0
    for end in ends:
        found = found | (block == end)
    return found


def first_block(ends, block):
    first = 0
    for end in ends:
        first = jnp.where(end <= block, end, first)
    return first


def summed_along(log_decay, chosen):
    heads = log_decay.shape[0]
    high = log_decay.astype(BF16)
    rest = log_decay - high.astype(F32)
    middle = rest.astype(BF16)
    low = (rest - middle.astype(F32)).astype(BF16)
    parts = jnp.concatenate([high, middle, low], axis=0)
    sums = jnp.dot(parts, chosen, preferred_element_type=F32)
    return sums[:heads] + sums[heads : 2 * heads] + sums[2 * heads :]


def state_kernel(
    lengths_hbm,
    input_hbm,
    write_hbm,
    decay_hbm,
    key_hbm,
    value_hbm,
    out_hbm,
    pair_hbm,
    out_ref,
    lengths_ref,
    input_ref,
    write_ref,
    decay_ref,
    pair_ref,
    sems,
    pair_sems,
    pair_out_sem,
    out_sems,
):
    heads, rows = decay_ref.shape
    copies = fetch(
        [(decay_hbm, decay_ref), (write_hbm, write_ref)]
        + column_pieces(input_hbm, input_ref)
        + [(lengths_hbm, lengths_ref)],
        sems,
    )
    keys = fetch(
        [(key_hbm, pair_ref.at[pl.ds(0, rows)]), (value_hbm, pair_ref.at[pl.ds(rows, rows)])],
        pair_sems,
    )
    copies[-1].wait()
    copies[0].wait()
    place = lax.axis_index("seq")
    ends = request_ends(lengths_ref)
    opens_0 = starts_request(ends, 2 * place)
    opens_1 = starts_request(ends, 2 * place + 1)
    log_decay = decay_ref[...]
    u = lax.broadcasted_iota(jnp.int32, (rows, rows), 0)
    j = lax.broadcasted_iota(jnp.int32, (rows, rows), 1)
    after = summed_along(log_decay, jnp.where(u > j, 1.0, 0.0).astype(BF16))
    total = after[:, :1] + log_decay[:, :1]
    token = lax.broadcasted_iota(jnp.int32, (heads, rows), 1)
    reaching = jnp.where((token < BLOCK) & opens_1, 0.0, jnp.exp(after))
    passing = jnp.where(opens_0 | opens_1, 0.0, jnp.exp(total))
    high = passing.astype(BF16).astype(F32)
    rest = passing - high
    middle = rest.astype(BF16).astype(F32)
    low = rest - middle
    line = lax.broadcasted_iota(jnp.int32, (EXTRA, 128), 0)
    for copy in keys:
        copy.wait()
    pair_out = pltpu.make_async_copy(pair_ref, pair_hbm, pair_out_sem)
    pair_out.start()
    copies[1].wait()
    writes = write_ref[...].astype(F32).T
    half = N // 2
    share = out_ref.shape[0] // PIECES
    started = [pair_out]
    for h in range(heads):
        if h % (heads // PIECES) == 0:
            copies[2 + h // (heads // PIECES)].wait()
        scaled = (writes * reaching[h : h + 1, :]).astype(BF16)
        state = jnp.dot(
            scaled, input_ref[:, h * P_SIZE : (h + 1) * P_SIZE], preferred_element_type=F32
        )
        tail = jnp.where(
            line == 0,
            high[h : h + 1, :],
            jnp.where(line == 1, middle[h : h + 1, :], jnp.where(line == 2, low[h : h + 1, :], 0.0)),
        )
        for part in range(2):
            out_ref[2 * h + part] = jnp.concatenate(
                [state[part * half : (part + 1) * half], tail], axis=0
            ).astype(BF16)
        if (h + 1) % (heads // PIECES) == 0:
            k = h // (heads // PIECES)
            at = pl.ds(k * share, share)
            copy = pltpu.make_async_copy(out_ref.at[at], out_hbm.at[at], out_sems.at[k])
            copy.start()
            started.append(copy)
    for copy in started:
        copy.wait()


def scan_kernel(states_ref, out_ref):
    count, rows, _ = out_ref.shape
    entering = jnp.zeros(out_ref.shape[1:], F32)
    for d in range(count):
        out_ref[d] = entering.astype(BF16)
        block = states_ref[d].astype(F32)
        passing = block[rows : rows + 1] + block[rows + 1 : rows + 2] + block[rows + 2 : rows + 3]
        entering = passing * entering + block[:rows]


def within_kernel(
    lengths_hbm,
    input_hbm,
    gate_hbm,
    write_hbm,
    read_hbm,
    decay_hbm,
    out_ref,
    lengths_ref,
    input_ref,
    gate_ref,
    write_ref,
    read_ref,
    decay_ref,
    sems,
):
    heads, rows = decay_ref.shape
    copies = fetch(
        [
            (lengths_hbm, lengths_ref),
            (decay_hbm, decay_ref),
            (write_hbm, write_ref),
            (read_hbm, read_ref),
        ]
        + column_pieces(input_hbm, input_ref)
        + column_pieces(gate_hbm, gate_ref),
        sems,
    )
    for copy in copies[:4]:
        copy.wait()
    place = lax.axis_index("seq")
    ends = request_ends(lengths_ref)
    opens_0 = starts_request(ends, 2 * place)
    opens_1 = starts_request(ends, 2 * place + 1)
    u = lax.broadcasted_iota(jnp.int32, (rows, rows), 0)
    j = lax.broadcasted_iota(jnp.int32, (rows, rows), 1)
    running = summed_along(decay_ref[...], jnp.where(u <= j, 1.0, 0.0).astype(BF16))
    down = running.T
    token = lax.broadcasted_iota(jnp.int32, (rows, heads), 0)
    cut = opens_0 | ((token >= BLOCK) & opens_1)
    entry = jnp.where(cut, 0.0, jnp.exp(down))
    affinity = lax.dot_general(
        read_ref[...], write_ref[...], (((1,), (1,)), ((), ())), preferred_element_type=F32
    )
    seen = (j <= u) & jnp.logical_not((u >= BLOCK) & (j < BLOCK) & opens_1)
    affinity = jnp.where(seen, affinity, 0.0)
    for h in range(heads):
        if h % (heads // PIECES) == 0:
            copies[4 + h // (heads // PIECES)].wait()
            copies[4 + PIECES + h // (heads // PIECES)].wait()
        columns = slice(h * P_SIZE, (h + 1) * P_SIZE)
        column = down[:, h : h + 1]
        line = running[h : h + 1, :]
        top = jnp.exp(jnp.minimum(column[:BLOCK] - line[:, :BLOCK], 0.0)) * affinity[:BLOCK, :BLOCK]
        bottom = jnp.exp(jnp.minimum(column[BLOCK:] - line, 0.0)) * affinity[BLOCK:]
        inputs = input_ref[:, columns]
        gate = gate_ref[:, columns].astype(F32)
        silu = gate / (1.0 + jnp.exp(-gate))
        out_ref[0, :BLOCK, columns] = (
            silu[:BLOCK]
            * jnp.dot(top.astype(BF16), inputs[:BLOCK], preferred_element_type=F32)
        ).astype(BF16)
        out_ref[0, BLOCK:, columns] = (
            silu[BLOCK:] * jnp.dot(bottom.astype(BF16), inputs, preferred_element_type=F32)
        ).astype(BF16)
        out_ref[1, :, columns] = (silu * entry[:, h : h + 1]).astype(BF16)


def mixed_kernel(within_ref, read_ref, entering_ref, gated_ref, squares_ref):
    _, rows, width = within_ref.shape
    heads = width // P_SIZE
    reads = read_ref[...]
    squares = jnp.zeros((rows, 2 * P_SIZE), F32)
    for h in range(0, heads, 2):
        columns = slice(h * P_SIZE, (h + 2) * P_SIZE)
        pair = jnp.concatenate(
            [
                jnp.concatenate([entering_ref[2 * k], entering_ref[2 * k + 1]], axis=0)
                for k in (h, h + 1)
            ],
            axis=1,
        )
        from_state = jnp.dot(reads, pair, preferred_element_type=F32)
        within = within_ref[0, :, columns].astype(F32)
        gated = within + within_ref[1, :, columns].astype(F32) * from_state
        gated_ref[:, columns] = gated
        squares = squares + gated * gated
    folded = squares[:, :P_SIZE] + squares[:, P_SIZE:]
    row = jnp.sum(folded.T, axis=0, keepdims=True)
    for k in range(squares_ref.shape[0]):
        squares_ref[k] = row


def scale_kernel(gated_ref, squares_ref, gain_ref, out_hbm, out_ref, sems):
    copies, _, rows = squares_ref.shape
    total = squares_ref[0]
    for k in range(1, copies):
        total = total + squares_ref[k]
    scaling = lax.rsqrt(total / (HEADS * P_SIZE) + 1e-05)
    column = jnp.broadcast_to(scaling, (128, rows)).T[:, :1]
    width = out_ref.shape[1] // PIECES
    started = []
    for k, (target, source) in enumerate(column_pieces(out_hbm, out_ref)):
        at = slice(k * width, (k + 1) * width)
        out_ref[:, at] = (gated_ref[:, at].astype(F32) * column * gain_ref[:, at]).astype(BF16)
        copy = pltpu.make_async_copy(source, target, sems.at[k])
        copy.start()
        started.append(copy)
    for copy in started:
        copy.wait()


def attention_kernel(steps, opens, closes, *refs):
    ins = 2 + len(steps) + (0 if opens else 2)
    outs = 1 if closes else 2
    sources, targets, refs = refs[:ins], refs[ins : ins + outs], refs[ins + outs :]
    held, results, sems, out_sems = refs[:ins], refs[ins : ins + outs], refs[-2], refs[-1]
    lengths_ref, query_ref = held[:2]
    pair_refs = held[2 : 2 + len(steps)]
    if not opens:
        summed_in_ref, kept_in_ref = held[-2:]
    for copy in fetch(list(zip(sources, held)), sems):
        copy.wait()
    started = []
    rows, width = query_ref.shape
    heads = width // HEAD_WIDTH
    place = lax.axis_index("seq")
    ends = request_ends(lengths_ref)
    scale = math.log2(math.e) / math.sqrt(HEAD_WIDTH)
    i = lax.broadcasted_iota(jnp.int32, (BLOCK, BLOCK), 0)
    j = lax.broadcasted_iota(jnp.int32, (BLOCK, BLOCK), 1)
    causal = jnp.where(j <= i, 0.0, -jnp.inf)
    firsts = [first_block(ends, 2 * place + a) for a in range(2)]

    def hidden(a, step, part):
        return jnp.where(2 * (place - step) + part >= firsts[a], 0.0, -jnp.inf)

    for g in range(heads):
        at = slice(g * HEAD_WIDTH, (g + 1) * HEAD_WIDTH)
        queries = query_ref[:, at]
        scores = [
            lax.dot_general(
                queries, pair[:rows, :], (((1,), (1,)), ((), ())), preferred_element_type=F32
            )
            for pair in pair_refs
        ]
        for a in range(2):
            down = slice(a * BLOCK, (a + 1) * BLOCK)
            tiles = []
            for k, step in enumerate(steps):
                for part in range(2):
                    if step == 0 and part > a:
                        continue
                    tile = scores[k][down, part * BLOCK : (part + 1) * BLOCK] * scale
                    tile = tile + (causal if step == 0 and part == a else hidden(a, step, part))
                    tiles.append((k, tile))
            largest = tiles[0][1]
            for _, tile in tiles[1:]:
                largest = jnp.maximum(largest, tile)
            largest = jnp.max(largest, axis=1, keepdims=True)
            if not opens:
                before = kept_in_ref[down, g : g + 1]
                largest = jnp.maximum(largest, before)
            weights = [(k, jnp.exp2(tile - largest)) for k, tile in tiles]
            total = weights[0][1]
            for _, weight in weights[1:]:
                total = total + weight
            total = jnp.sum(total, axis=1, keepdims=True)
            summed = None
            if not opens:
                kept = jnp.exp2(before - largest)
                total = total + kept * kept_in_ref[down, heads + g : heads + g + 1]
                summed = kept * summed_in_ref[down, at]
            for k in range(len(steps)):
                mine = [weight.astype(BF16) for m, weight in weights if m == k]
                values = pair_refs[k][rows : rows + BLOCK * len(mine), :]
                term = jnp.dot(
                    jnp.concatenate(mine, axis=1), values, preferred_element_type=F32
                )
                summed = term if summed is None else summed + term
            if closes:
                results[0][down, at] = (summed / total).astype(BF16)
            else:
                results[0][down, at] = summed
                results[1][down, g : g + 1] = largest
                results[1][down, heads + g : heads + g + 1] = total
        columns = pl.ds(g * HEAD_WIDTH, HEAD_WIDTH)
        copy = pltpu.make_async_copy(
            results[0].at[:, columns], targets[0].at[:, columns], out_sems.at[g]
        )
        copy.start()
        started.append(copy)
    if not closes:
        copy = pltpu.make_async_copy(results[1], targets[1], out_sems.at[heads])
        copy.start()
        started.append(copy)
    for copy in started:
        copy.wait()


def call(
    kernel, ins, outs, limit, flops=0, nbytes=0, transcendentals=0, name=None, places=None, scratch=()
):
    return pl.pallas_call(
        kernel,
        in_specs=ins,
        out_specs=places or jax.tree.map(lambda _: VMEM, outs),
        out_shape=outs,
        scratch_shapes=list(scratch),
        compiler_params=pltpu.CompilerParams(vmem_limit_bytes=limit * MIB),
        cost_estimate=pl.CostEstimate(
            flops=flops, bytes_accessed=nbytes, transcendentals=transcendentals
        ),
        name=name,
    )


def shifted(shard, by):
    count = lax.axis_size("seq")
    return lax.ppermute(shard, "seq", [(i, (i + by) % count) for i in range(count)])


def on_device(
    mixer_input,
    mixer_gate,
    state_write,
    state_read,
    log_decay,
    norm_gain,
    queries,
    key_matrix_rows,
    value_matrix_rows,
    request_blocks,
):
    rows, width = mixer_input.shape
    count = lax.axis_size("seq")
    copies = lax.axis_size("tp")
    part = width // P_SIZE * N // count
    shape = jax.ShapeDtypeStruct

    lengths = pltpu.SMEM(request_blocks.shape, jnp.int32)
    whole = pltpu.VMEM((rows, width), BF16)
    states, own_pair = call(
        state_kernel,
        [HBM] * 6,
        (
            shape((count, part + EXTRA, P_SIZE), BF16),
            shape((2 * rows, HEAD_WIDTH), BF16),
        ),
        60,
        flops=2 * rows * width * N,
        nbytes=2 * rows * width,
        name="states",
        places=(HBM, HBM),
        scratch=[
            pltpu.VMEM((count, part + EXTRA, P_SIZE), BF16),
            lengths,
            whole,
            pltpu.VMEM((rows, N), BF16),
            pltpu.VMEM(log_decay.shape, F32),
            pltpu.VMEM((2 * rows, HEAD_WIDTH), BF16),
            pltpu.SemaphoreType.DMA((3 + PIECES,)),
            pltpu.SemaphoreType.DMA((2,)),
            pltpu.SemaphoreType.DMA,
            pltpu.SemaphoreType.DMA((PIECES,)),
        ],
    )(request_blocks, mixer_input, state_write, log_decay, key_matrix_rows, value_matrix_rows)
    behind_1 = shifted(own_pair, 1)
    behind_4 = shifted(own_pair, 4)
    states = lax.all_to_all(states, "seq", 0, 0)

    pair = pltpu.VMEM(own_pair.shape, BF16)
    query = pltpu.VMEM(queries.shape, BF16)
    partly = [pltpu.VMEM(queries.shape, F32), pltpu.VMEM((rows, 128), F32)]
    sums = queries.shape[1] // HEAD_WIDTH + 1
    summed, kept = call(
        partial(attention_kernel, (0, 1, 4), True, False),
        [HBM] * 5,
        (shape(queries.shape, F32), shape((rows, 128), F32)),
        60,
        flops=64 * rows * 3 * rows * queries.shape[1],
        nbytes=4 * rows * queries.shape[1],
        transcendentals=8 * rows * 3 * rows,
        name="attention_near",
        places=(HBM, HBM),
        scratch=[lengths, query, pair, pair, pair]
        + partly
        + [pltpu.SemaphoreType.DMA((5,)), pltpu.SemaphoreType.DMA((sums,))],
    )(request_blocks, queries, own_pair, behind_1, behind_4)
    states, summed, kept = lax.optimization_barrier((states, summed, kept))

    entering = call(
        scan_kernel,
        [VMEM],
        shape((count, part, P_SIZE), BF16),
        8,
        flops=2 * count * part * P_SIZE,
        nbytes=4 * count * part * P_SIZE,
        name="scan",
    )(states)
    entering = lax.all_to_all(entering, "seq", 0, 0)

    behind_2 = shifted(behind_1, 1)
    behind_3 = shifted(behind_4, -1)
    within = call(
        within_kernel,
        [HBM] * 6,
        shape((2, rows, width), BF16),
        60,
        flops=2 * rows * rows * width,
        nbytes=12 * rows * width,
        transcendentals=3 * rows * width,
        name="within",
        scratch=[
            lengths,
            whole,
            whole,
            pltpu.VMEM((rows, N), BF16),
            pltpu.VMEM((rows, N), BF16),
            pltpu.VMEM(log_decay.shape, F32),
            pltpu.SemaphoreType.DMA((4 + 2 * PIECES,)),
        ],
    )(request_blocks, mixer_input, mixer_gate, state_write, state_read, log_decay)

    attention_out = call(
        partial(attention_kernel, (2, 3), False, True),
        [HBM] * 6,
        shape(queries.shape, BF16),
        60,
        flops=64 * rows * 3 * rows * queries.shape[1],
        nbytes=8 * rows * queries.shape[1],
        transcendentals=8 * rows * 2 * rows,
        name="attention_far",
        places=HBM,
        scratch=[lengths, query, pair, pair]
        + partly
        + [query, pltpu.SemaphoreType.DMA((6,)), pltpu.SemaphoreType.DMA((sums,))],
    )(request_blocks, queries, behind_2, behind_3, summed, kept)
    entering, attention_out = lax.optimization_barrier((entering, attention_out))

    gated, squares = call(
        mixed_kernel,
        [VMEM] * 3,
        (shape((rows, width), F32), shape((copies, 1, rows), F32)),
        8,
        flops=2 * rows * N * width,
        nbytes=12 * rows * width,
        name="mixed",
    )(within, state_read, entering)
    squares = lax.all_to_all(squares, "tp", 0, 0)

    mixer_out = call(
        scale_kernel,
        [VMEM] * 3,
        shape((rows, width), BF16),
        8,
        flops=2 * rows * width,
        nbytes=6 * rows * width,
        name="scaled",
        places=HBM,
        scratch=[whole, pltpu.SemaphoreType.DMA((PIECES,))],
    )(gated, squares, norm_gain[None, :])
    return (mixer_out, attention_out)


def solution(mesh):
    placed = (
        P("seq", "tp"),
        P("seq", "tp"),
        P("seq", None),
        P("seq", None),
        P("tp", "seq"),
        P("tp"),
        P("seq", "tp"),
        P("seq", "tp"),
        P("seq", "tp"),
        P(),
    )
    return jax.shard_map(
        on_device,
        mesh=mesh,
        in_specs=placed,
        out_specs=(P("seq", "tp"), P("seq", "tp")),
        check_vma=False,
    )
```

```python
from functools import partial
import math

import jax
import jax.numpy as jnp
from jax import lax
from jax.experimental import pallas as pl
from jax.experimental.pallas import tpu as pltpu
from jax.sharding import PartitionSpec as P

HEADS = 128
P_SIZE = 128
N = 128
HEAD_WIDTH = 128
BLOCK = 128
EXTRA = 8
F32 = jnp.float32
BF16 = jnp.bfloat16
VMEM = pl.BlockSpec(memory_space=pltpu.VMEM)
HBM = pl.BlockSpec(memory_space=pltpu.HBM)
SMEM = pl.BlockSpec(memory_space=pltpu.SMEM)
MIB = 1024 * 1024
PIECES = 2


def fetch(pairs, sems):
    copies = [
        pltpu.make_async_copy(source, target, sems.at[k]) for k, (source, target) in enumerate(pairs)
    ]
    for copy in copies:
        copy.start()
    return copies


def column_pieces(source, target):
    width = target.shape[1] // PIECES
    columns = [pl.ds(k * width, width) for k in range(PIECES)]
    return [(source.at[:, at], target.at[:, at]) for at in columns]


def request_ends(lengths_ref):
    ends = []
    total = 0
    for r in range(lengths_ref.shape[0]):
        total = total + lengths_ref[r]
        ends.append(total)
    return ends


def starts_request(ends, block):
    found = block == 0
    for end in ends:
        found = found | (block == end)
    return found


def first_block(ends, block):
    first = 0
    for end in ends:
        first = jnp.where(end <= block, end, first)
    return first


def summed_along(log_decay, chosen):
    heads = log_decay.shape[0]
    high = log_decay.astype(BF16)
    rest = log_decay - high.astype(F32)
    middle = rest.astype(BF16)
    low = (rest - middle.astype(F32)).astype(BF16)
    parts = jnp.concatenate([high, middle, low], axis=0)
    sums = jnp.dot(parts, chosen, preferred_element_type=F32)
    return sums[:heads] + sums[heads : 2 * heads] + sums[2 * heads :]


def state_kernel(
    lengths_hbm,
    input_hbm,
    write_hbm,
    decay_hbm,
    key_hbm,
    value_hbm,
    out_hbm,
    pair_hbm,
    out_ref,
    lengths_ref,
    input_ref,
    write_ref,
    decay_ref,
    pair_ref,
    sems,
    pair_sems,
    pair_out_sem,
    out_sems,
):
    heads, rows = decay_ref.shape
    copies = fetch(
        [(decay_hbm, decay_ref), (write_hbm, write_ref)]
        + column_pieces(input_hbm, input_ref)
        + [(lengths_hbm, lengths_ref)],
        sems,
    )
    keys = fetch(
        [(key_hbm, pair_ref.at[pl.ds(0, rows)]), (value_hbm, pair_ref.at[pl.ds(rows, rows)])],
        pair_sems,
    )
    copies[-1].wait()
    copies[0].wait()
    place = lax.axis_index("seq")
    ends = request_ends(lengths_ref)
    opens_0 = starts_request(ends, 2 * place)
    opens_1 = starts_request(ends, 2 * place + 1)
    log_decay = decay_ref[...]
    u = lax.broadcasted_iota(jnp.int32, (rows, rows), 0)
    j = lax.broadcasted_iota(jnp.int32, (rows, rows), 1)
    after = summed_along(log_decay, jnp.where(u > j, 1.0, 0.0).astype(BF16))
    total = after[:, :1] + log_decay[:, :1]
    token = lax.broadcasted_iota(jnp.int32, (heads, rows), 1)
    reaching = jnp.where((token < BLOCK) & opens_1, 0.0, jnp.exp(after))
    passing = jnp.where(opens_0 | opens_1, 0.0, jnp.exp(total))
    high = passing.astype(BF16).astype(F32)
    rest = passing - high
    middle = rest.astype(BF16).astype(F32)
    low = rest - middle
    line = lax.broadcasted_iota(jnp.int32, (EXTRA, 128), 0)
    for copy in keys:
        copy.wait()
    pair_out = pltpu.make_async_copy(pair_ref, pair_hbm, pair_out_sem)
    pair_out.start()
    copies[1].wait()
    writes = write_ref[...].astype(F32).T
    half = N // 2
    share = out_ref.shape[0] // PIECES
    started = [pair_out]
    for h in range(heads):
        if h % (heads // PIECES) == 0:
            copies[2 + h // (heads // PIECES)].wait()
        scaled = (writes * reaching[h : h + 1, :]).astype(BF16)
        state = jnp.dot(
            scaled, input_ref[:, h * P_SIZE : (h + 1) * P_SIZE], preferred_element_type=F32
        )
        tail = jnp.where(
            line == 0,
            high[h : h + 1, :],
            jnp.where(line == 1, middle[h : h + 1, :], jnp.where(line == 2, low[h : h + 1, :], 0.0)),
        )
        for part in range(2):
            out_ref[2 * h + part] = jnp.concatenate(
                [state[part * half : (part + 1) * half], tail], axis=0
            ).astype(BF16)
        if (h + 1) % (heads // PIECES) == 0:
            k = h // (heads // PIECES)
            at = pl.ds(k * share, share)
            copy = pltpu.make_async_copy(out_ref.at[at], out_hbm.at[at], out_sems.at[k])
            copy.start()
            started.append(copy)
    for copy in started:
        copy.wait()


def scan_kernel(states_ref, out_ref):
    count, rows, _ = out_ref.shape
    entering = jnp.zeros(out_ref.shape[1:], F32)
    for d in range(count):
        out_ref[d] = entering.astype(BF16)
        block = states_ref[d].astype(F32)
        passing = block[rows : rows + 1] + block[rows + 1 : rows + 2] + block[rows + 2 : rows + 3]
        entering = passing * entering + block[:rows]


def within_kernel(
    lengths_hbm,
    input_hbm,
    gate_hbm,
    write_hbm,
    read_hbm,
    decay_hbm,
    out_ref,
    lengths_ref,
    input_ref,
    gate_ref,
    write_ref,
    read_ref,
    decay_ref,
    sems,
):
    heads, rows = decay_ref.shape
    copies = fetch(
        [
            (lengths_hbm, lengths_ref),
            (decay_hbm, decay_ref),
            (write_hbm, write_ref),
            (read_hbm, read_ref),
        ]
        + column_pieces(input_hbm, input_ref)
        + column_pieces(gate_hbm, gate_ref),
        sems,
    )
    for copy in copies[:4]:
        copy.wait()
    place = lax.axis_index("seq")
    ends = request_ends(lengths_ref)
    opens_0 = starts_request(ends, 2 * place)
    opens_1 = starts_request(ends, 2 * place + 1)
    u = lax.broadcasted_iota(jnp.int32, (rows, rows), 0)
    j = lax.broadcasted_iota(jnp.int32, (rows, rows), 1)
    running = summed_along(decay_ref[...], jnp.where(u <= j, 1.0, 0.0).astype(BF16))
    down = running.T
    token = lax.broadcasted_iota(jnp.int32, (rows, heads), 0)
    cut = opens_0 | ((token >= BLOCK) & opens_1)
    entry = jnp.where(cut, 0.0, jnp.exp(down))
    affinity = lax.dot_general(
        read_ref[...], write_ref[...], (((1,), (1,)), ((), ())), preferred_element_type=F32
    )
    seen = (j <= u) & jnp.logical_not((u >= BLOCK) & (j < BLOCK) & opens_1)
    affinity = jnp.where(seen, affinity, 0.0)
    for h in range(heads):
        if h % (heads // PIECES) == 0:
            copies[4 + h // (heads // PIECES)].wait()
            copies[4 + PIECES + h // (heads // PIECES)].wait()
        columns = slice(h * P_SIZE, (h + 1) * P_SIZE)
        column = down[:, h : h + 1]
        line = running[h : h + 1, :]
        top = jnp.exp(jnp.minimum(column[:BLOCK] - line[:, :BLOCK], 0.0)) * affinity[:BLOCK, :BLOCK]
        bottom = jnp.exp(jnp.minimum(column[BLOCK:] - line, 0.0)) * affinity[BLOCK:]
        inputs = input_ref[:, columns]
        gate = gate_ref[:, columns].astype(F32)
        silu = gate / (1.0 + jnp.exp(-gate))
        out_ref[0, :BLOCK, columns] = (
            silu[:BLOCK]
            * jnp.dot(top.astype(BF16), inputs[:BLOCK], preferred_element_type=F32)
        ).astype(BF16)
        out_ref[0, BLOCK:, columns] = (
            silu[BLOCK:] * jnp.dot(bottom.astype(BF16), inputs, preferred_element_type=F32)
        ).astype(BF16)
        out_ref[1, :, columns] = (silu * entry[:, h : h + 1]).astype(BF16)


def mixed_kernel(within_ref, read_ref, entering_ref, gated_ref, squares_ref):
    _, rows, width = within_ref.shape
    heads = width // P_SIZE
    reads = read_ref[...]
    squares = jnp.zeros((rows, 2 * P_SIZE), F32)
    for h in range(0, heads, 2):
        columns = slice(h * P_SIZE, (h + 2) * P_SIZE)
        pair = jnp.concatenate(
            [
                jnp.concatenate([entering_ref[2 * k], entering_ref[2 * k + 1]], axis=0)
                for k in (h, h + 1)
            ],
            axis=1,
        )
        from_state = jnp.dot(reads, pair, preferred_element_type=F32)
        within = within_ref[0, :, columns].astype(F32)
        gated = within + within_ref[1, :, columns].astype(F32) * from_state
        gated_ref[:, columns] = gated
        squares = squares + gated * gated
    folded = squares[:, :P_SIZE] + squares[:, P_SIZE:]
    row = jnp.sum(folded.T, axis=0, keepdims=True)
    for k in range(squares_ref.shape[0]):
        squares_ref[k] = row


def scale_kernel(gated_ref, squares_ref, gain_ref, out_hbm, out_ref, sems):
    copies, _, rows = squares_ref.shape
    total = squares_ref[0]
    for k in range(1, copies):
        total = total + squares_ref[k]
    scaling = lax.rsqrt(total / (HEADS * P_SIZE) + 1e-05)
    column = jnp.broadcast_to(scaling, (128, rows)).T[:, :1]
    width = out_ref.shape[1] // PIECES
    started = []
    for k, (target, source) in enumerate(column_pieces(out_hbm, out_ref)):
        at = slice(k * width, (k + 1) * width)
        out_ref[:, at] = (gated_ref[:, at].astype(F32) * column * gain_ref[:, at]).astype(BF16)
        copy = pltpu.make_async_copy(source, target, sems.at[k])
        copy.start()
        started.append(copy)
    for copy in started:
        copy.wait()


def attention_kernel(steps, opens, closes, *refs):
    ins = 2 + len(steps) + (0 if opens else 2)
    outs = 1 if closes else 2
    sources, targets, refs = refs[:ins], refs[ins : ins + outs], refs[ins + outs :]
    held, results, sems, out_sems = refs[:ins], refs[ins : ins + outs], refs[-2], refs[-1]
    lengths_ref, query_ref = held[:2]
    pair_refs = held[2 : 2 + len(steps)]
    if not opens:
        summed_in_ref, kept_in_ref = held[-2:]
    for copy in fetch(list(zip(sources, held)), sems):
        copy.wait()
    started = []
    rows, width = query_ref.shape
    heads = width // HEAD_WIDTH
    place = lax.axis_index("seq")
    ends = request_ends(lengths_ref)
    scale = math.log2(math.e) / math.sqrt(HEAD_WIDTH)
    i = lax.broadcasted_iota(jnp.int32, (BLOCK, BLOCK), 0)
    j = lax.broadcasted_iota(jnp.int32, (BLOCK, BLOCK), 1)
    causal = jnp.where(j <= i, 0.0, -jnp.inf)
    firsts = [first_block(ends, 2 * place + a) for a in range(2)]

    def hidden(a, step, part):
        return jnp.where(2 * (place - step) + part >= firsts[a], 0.0, -jnp.inf)

    for g in range(heads):
        at = slice(g * HEAD_WIDTH, (g + 1) * HEAD_WIDTH)
        queries = query_ref[:, at]
        scores = [
            lax.dot_general(
                queries, pair[:rows, :], (((1,), (1,)), ((), ())), preferred_element_type=F32
            )
            for pair in pair_refs
        ]
        for a in range(2):
            down = slice(a * BLOCK, (a + 1) * BLOCK)
            tiles = []
            for k, step in enumerate(steps):
                for part in range(2):
                    if step == 0 and part > a:
                        continue
                    tile = scores[k][down, part * BLOCK : (part + 1) * BLOCK] * scale
                    tile = tile + (causal if step == 0 and part == a else hidden(a, step, part))
                    tiles.append((k, tile))
            largest = tiles[0][1]
            for _, tile in tiles[1:]:
                largest = jnp.maximum(largest, tile)
            largest = jnp.max(largest, axis=1, keepdims=True)
            if not opens:
                before = kept_in_ref[down, g : g + 1]
                largest = jnp.maximum(largest, before)
            weights = [(k, jnp.exp2(tile - largest)) for k, tile in tiles]
            total = weights[0][1]
            for _, weight in weights[1:]:
                total = total + weight
            total = jnp.sum(total, axis=1, keepdims=True)
            summed = None
            if not opens:
                kept = jnp.exp2(before - largest)
                total = total + kept * kept_in_ref[down, heads + g : heads + g + 1]
                summed = kept * summed_in_ref[down, at]
            for k in range(len(steps)):
                mine = [weight.astype(BF16) for m, weight in weights if m == k]
                values = pair_refs[k][rows : rows + BLOCK * len(mine), :]
                term = jnp.dot(
                    jnp.concatenate(mine, axis=1), values, preferred_element_type=F32
                )
                summed = term if summed is None else summed + term
            if closes:
                results[0][down, at] = (summed / total).astype(BF16)
            else:
                results[0][down, at] = summed
                results[1][down, g : g + 1] = largest
                results[1][down, heads + g : heads + g + 1] = total
        columns = pl.ds(g * HEAD_WIDTH, HEAD_WIDTH)
        copy = pltpu.make_async_copy(
            results[0].at[:, columns], targets[0].at[:, columns], out_sems.at[g]
        )
        copy.start()
        started.append(copy)
    if not closes:
        copy = pltpu.make_async_copy(results[1], targets[1], out_sems.at[heads])
        copy.start()
        started.append(copy)
    for copy in started:
        copy.wait()


def call(
    kernel, ins, outs, limit, flops=0, nbytes=0, transcendentals=0, name=None, places=None, scratch=()
):
    return pl.pallas_call(
        kernel,
        in_specs=ins,
        out_specs=places or jax.tree.map(lambda _: VMEM, outs),
        out_shape=outs,
        scratch_shapes=list(scratch),
        compiler_params=pltpu.CompilerParams(vmem_limit_bytes=limit * MIB),
        cost_estimate=pl.CostEstimate(
            flops=flops, bytes_accessed=nbytes, transcendentals=transcendentals
        ),
        name=name,
    )


def shifted(shard, by):
    count = lax.axis_size("seq")
    return lax.ppermute(shard, "seq", [(i, (i + by) % count) for i in range(count)])


def on_device(
    mixer_input,
    mixer_gate,
    state_write,
    state_read,
    log_decay,
    norm_gain,
    queries,
    key_matrix_rows,
    value_matrix_rows,
    request_blocks,
):
    rows, width = mixer_input.shape
    count = lax.axis_size("seq")
    copies = lax.axis_size("tp")
    part = width // P_SIZE * N // count
    shape = jax.ShapeDtypeStruct

    lengths = pltpu.SMEM(request_blocks.shape, jnp.int32)
    whole = pltpu.VMEM((rows, width), BF16)
    states, own_pair = call(
        state_kernel,
        [HBM] * 6,
        (
            shape((count, part + EXTRA, P_SIZE), BF16),
            shape((2 * rows, HEAD_WIDTH), BF16),
        ),
        60,
        flops=2 * rows * width * N,
        nbytes=2 * rows * width,
        name="states",
        places=(HBM, HBM),
        scratch=[
            pltpu.VMEM((count, part + EXTRA, P_SIZE), BF16),
            lengths,
            whole,
            pltpu.VMEM((rows, N), BF16),
            pltpu.VMEM(log_decay.shape, F32),
            pltpu.VMEM((2 * rows, HEAD_WIDTH), BF16),
            pltpu.SemaphoreType.DMA((3 + PIECES,)),
            pltpu.SemaphoreType.DMA((2,)),
            pltpu.SemaphoreType.DMA,
            pltpu.SemaphoreType.DMA((PIECES,)),
        ],
    )(request_blocks, mixer_input, state_write, log_decay, key_matrix_rows, value_matrix_rows)
    behind_1 = shifted(own_pair, 1)
    behind_4 = shifted(own_pair, 4)
    states = lax.all_to_all(states, "seq", 0, 0)

    pair = pltpu.VMEM(own_pair.shape, BF16)
    query = pltpu.VMEM(queries.shape, BF16)
    partly = [pltpu.VMEM(queries.shape, F32), pltpu.VMEM((rows, 128), F32)]
    sums = queries.shape[1] // HEAD_WIDTH + 1
    summed, kept = call(
        partial(attention_kernel, (0, 1, 4), True, False),
        [HBM] * 5,
        (shape(queries.shape, F32), shape((rows, 128), F32)),
        60,
        flops=64 * rows * 3 * rows * queries.shape[1],
        nbytes=4 * rows * queries.shape[1],
        transcendentals=8 * rows * 3 * rows,
        name="attention_near",
        places=(HBM, HBM),
        scratch=[lengths, query, pair, pair, pair]
        + partly
        + [pltpu.SemaphoreType.DMA((5,)), pltpu.SemaphoreType.DMA((sums,))],
    )(request_blocks, queries, own_pair, behind_1, behind_4)
    states, summed, kept = lax.optimization_barrier((states, summed, kept))

    entering = call(
        scan_kernel,
        [VMEM],
        shape((count, part, P_SIZE), BF16),
        8,
        flops=2 * count * part * P_SIZE,
        nbytes=4 * count * part * P_SIZE,
        name="scan",
    )(states)
    entering = lax.all_to_all(entering, "seq", 0, 0)

    behind_2 = shifted(behind_1, 1)
    behind_3 = shifted(behind_4, -1)
    within = call(
        within_kernel,
        [HBM] * 6,
        shape((2, rows, width), BF16),
        60,
        flops=2 * rows * rows * width,
        nbytes=12 * rows * width,
        transcendentals=3 * rows * width,
        name="within",
        scratch=[
            lengths,
            whole,
            whole,
            pltpu.VMEM((rows, N), BF16),
            pltpu.VMEM((rows, N), BF16),
            pltpu.VMEM(log_decay.shape, F32),
            pltpu.SemaphoreType.DMA((4 + 2 * PIECES,)),
        ],
    )(request_blocks, mixer_input, mixer_gate, state_write, state_read, log_decay)

    attention_out = call(
        partial(attention_kernel, (2, 3), False, True),
        [HBM] * 6,
        shape(queries.shape, BF16),
        60,
        flops=64 * rows * 3 * rows * queries.shape[1],
        nbytes=8 * rows * queries.shape[1],
        transcendentals=8 * rows * 2 * rows,
        name="attention_far",
        places=HBM,
        scratch=[lengths, query, pair, pair]
        + partly
        + [query, pltpu.SemaphoreType.DMA((6,)), pltpu.SemaphoreType.DMA((sums,))],
    )(request_blocks, queries, behind_2, behind_3, summed, kept)
    entering, attention_out = lax.optimization_barrier((entering, attention_out))

    gated, squares = call(
        mixed_kernel,
        [VMEM] * 3,
        (shape((rows, width), F32), shape((copies, 1, rows), F32)),
        8,
        flops=2 * rows * N * width,
        nbytes=12 * rows * width,
        name="mixed",
    )(within, state_read, entering)
    squares = lax.all_to_all(squares, "tp", 0, 0)

    mixer_out = call(
        scale_kernel,
        [VMEM] * 3,
        shape((rows, width), BF16),
        8,
        flops=2 * rows * width,
        nbytes=6 * rows * width,
        name="scaled",
        places=HBM,
        scratch=[whole, pltpu.SemaphoreType.DMA((PIECES,))],
    )(gated, squares, norm_gain[None, :])
    return (mixer_out, attention_out)


def solution(mesh):
    placed = (
        P("seq", "tp"),
        P("seq", "tp"),
        P("seq", None),
        P("seq", None),
        P("tp", "seq"),
        P("tp"),
        P("seq", "tp"),
        P("seq", "tp"),
        P("seq", "tp"),
        P(),
    )
    return jax.shard_map(
        on_device,
        mesh=mesh,
        in_specs=placed,
        out_specs=(P("seq", "tp"), P("seq", "tp")),
        check_vma=False,
    )
```
